32 devices in a mesh: grp: 8 (over y, x, core), sub: 4 (over z).
Axes of the slice: x: 2, y: 2, z: 4, core: 2. Of those that a mesh axis runs over, the one named last changes fastest.
Arguments:
- eigvecs: bfloat16 [8, 4, 32, 3072], P('grp', 'sub'), may hold values from -1 to 1
- local_blocks: bfloat16 [8, 4, 32, 7, 4096], P('grp', 'sub'), may hold values from -0.25 to 0.25
- local_cols: int32 [8, 4, 32, 7], P('grp', 'sub'), may hold values from 0 to 31
- margin_rows: int32 [8, 4, 4, 256], P('grp', 'sub'), may hold values from 0 to 511
- margin_lens: int32 [8, 4, 4], P('grp', 'sub'), may hold values from 1 to 256
- peer_blocks: bfloat16 [8, 4, 4, 4, 4096], P('grp', 'sub'), may hold values from -0.75 to 0.75
- peer_rowblocks: int32 [8, 4, 4, 4], P('grp', 'sub'), may hold values from 0 to 31
- cross_blocks: bfloat16 [8, 4, 2, 2, 4096], P('grp', 'sub'), may hold values from -0.75 to 0.75
- cross_rowblocks: int32 [8, 4, 2, 2], P('grp', 'sub'), may hold values from 0 to 31
Outputs:
- group_matrix: float32 [8, 192, 192], P('grp')
- cross_rows: float32 [8, 4, 2, 48, 48], P('grp', 'sub')
The draws below stay inside these ranges and needn't reach their ends.
All inputs are finite; a program needn't handle non-finite values.
Results may differ from the reference program's by a relative error of at most 0.0029.
Values may be sent and summed in bfloat16 or wider, within the bound.
A program may use at most 64 MiB of HBM per device.

```python
import jax
import jax.numpy as jnp
from jax import lax

K = 48
NBLK = 32
NNZ = 7
BND = 512
CAP = 256
FACE = 128
NCB = 4
NFB = 2
PEERS = 4
GROUPS = 8


def touch_ends(result, stream_key, smallest, high):
    longest = result.shape.index(max(result.shape))
    spots = []
    for shift in (0, 1):
        where = [jax.random.randint(jax.random.fold_in(stream_key, axis), (), 0, length) for axis, length in enumerate(result.shape)]
        where[longest] = (where[longest] + shift) % result.shape[longest]
        spots.append(tuple(where))
    return result.at[spots[0]].set(smallest).at[spots[1]].set(high)


def levels(rng, extent, pieces, low, top_value):
    level = 1.0
    for dim, blocks in pieces:
        heights = jax.random.uniform(jax.random.fold_in(jax.random.fold_in(rng, 6), dim), (blocks,), jnp.float32, low / len(pieces), top_value / len(pieces))
        level = level * jnp.repeat(jnp.exp(heights), extent[dim] // blocks).reshape((-1,) + (1,) * (len(extent) - 1 - dim))
    return level


def gaussian(stream_key, shape, scale, bound, split=(), kind=jnp.bfloat16):
    factor_of = levels(stream_key, shape, split, -0.22, 0.18) if split else 1.0
    values = jax.random.normal(stream_key, shape, jnp.float32) * scale * factor_of
    return jnp.minimum(jnp.maximum(values, -bound), bound).astype(kind)


def setup_inputs(seed: int = 0) -> dict:
    streams_of = jax.random.split(jax.random.key(seed), 10)
    eigvecs = gaussian(streams_of[0], (GROUPS, PEERS, NBLK, K * 64), 0.125, 1.0, ((0, 8), (1, 4)))
    local_blocks = gaussian(streams_of[1], (GROUPS, PEERS, NBLK, NNZ, 4096), (NNZ * 64) ** -0.5, 0.25, ((0, 8), (1, 4)))
    local_cols = touch_ends(jax.random.randint(streams_of[2], (GROUPS, PEERS, NBLK, NNZ), 0, NBLK), jax.random.fold_in(streams_of[2], 1), 0, NBLK - 1).astype(jnp.int32)
    margin_rows = touch_ends(jax.random.randint(streams_of[3], (GROUPS, PEERS, PEERS, CAP), 0, BND), jax.random.fold_in(streams_of[3], 1), 0, BND - 1).astype(jnp.int32)
    margin_lens = touch_ends(jax.random.randint(streams_of[4], (GROUPS, PEERS, PEERS), 1, CAP + 1), jax.random.fold_in(streams_of[4], 1), 1, CAP).astype(jnp.int32)
    peer_blocks = gaussian(streams_of[5], (GROUPS, PEERS, PEERS, NCB, 4096), 64 ** -0.5, 0.75, ((0, 8), (1, 4)))
    peer_rowblocks = touch_ends(jax.random.randint(streams_of[6], (GROUPS, PEERS, PEERS, NCB), 0, NBLK), jax.random.fold_in(streams_of[6], 1), 0, NBLK - 1).astype(jnp.int32)
    cross_blocks = gaussian(streams_of[7], (GROUPS, PEERS, 2, NFB, 4096), 64 ** -0.5, 0.75, ((0, 8), (1, 4)))
    cross_rowblocks = touch_ends(jax.random.randint(streams_of[8], (GROUPS, PEERS, 2, NFB), 0, NBLK), jax.random.fold_in(streams_of[8], 1), 0, NBLK - 1).astype(jnp.int32)
    return {"eigvecs": eigvecs, "local_blocks": local_blocks, "local_cols": local_cols, "margin_rows": margin_rows, "margin_lens": margin_lens, "peer_blocks": peer_blocks, "peer_rowblocks": peer_rowblocks, "cross_blocks": cross_blocks, "cross_rowblocks": cross_rowblocks}


def diag_term(vec_rows, blocks, cols):
    num_blocks = vec_rows.shape[0]
    picked = vec_rows[cols].reshape(num_blocks, cols.shape[1], K, 64)
    blocks_sq = blocks.reshape(num_blocks, cols.shape[1], 64, 64)
    applied = jnp.einsum("rsij,rskj->rki", blocks_sq.astype(jnp.float32), picked.astype(jnp.float32))
    applied = applied.astype(jnp.bfloat16)
    own_vec = vec_rows.reshape(num_blocks, K, 64)
    return jnp.einsum("rkc,rlc->kl", own_vec.astype(jnp.float32), applied.astype(jnp.float32))


def couple(vec_rows, received, blocks, rowblocks):
    num_slots, num_col = rowblocks.shape
    local_part = vec_rows[rowblocks].reshape(num_slots, num_col, K, 64)
    blocks_sq = blocks.reshape(num_slots, num_col, 64, 64)
    mixed_part = jnp.einsum("pcki,pcij->pckj", local_part.astype(jnp.float32), blocks_sq.astype(jnp.float32)).astype(jnp.bfloat16)
    remote_part = received.reshape(num_slots, num_col, K, 64)
    return jnp.einsum("pckj,pclj->pkl", mixed_part.astype(jnp.float32), remote_part.astype(jnp.float32))


def reference(eigvecs, local_blocks, local_cols, margin_rows, margin_lens, peer_blocks, peer_rowblocks, cross_blocks, cross_rowblocks):
    subs = eigvecs.shape[1]
    layer_blocks = BND // 64
    face_blocks = FACE // 64
    zero_face = jnp.zeros((1, subs, face_blocks, K * 64), jnp.bfloat16)
    lower = eigvecs[:, :, layer_blocks:layer_blocks + face_blocks]
    upper = eigvecs[:, :, layer_blocks + face_blocks:layer_blocks + 2 * face_blocks]
    from_prev = jnp.concatenate([zero_face, upper[:-1]], axis=0)
    from_next = jnp.concatenate([lower[1:], zero_face], axis=0)
    across = jnp.stack([from_prev, from_next], axis=2)
    slot_ids = jnp.arange(subs, dtype=jnp.int32)
    cell_ids = jnp.arange(CAP, dtype=jnp.int32)

    def one_group(group_items):
        vec_group, blk_group, col_group, row_group, span_group, pb_group, pr_group, cb_group, cr_group, face_group = group_items
        layers = vec_group[:, :layer_blocks].reshape(subs, layer_blocks, K, 64)
        layers = jnp.transpose(layers, (0, 2, 1, 3)).reshape(subs, K, BND)

        def one_sub(vec_rows, blocks, cols, want_rows, spans, p_blocks, p_rows, c_blocks, c_rows, faces, own_slot):
            received = jnp.take_along_axis(layers, want_rows[:, None, :], axis=2)
            live_mask = (cell_ids[None, :] < spans[:, None]) & (slot_ids[:, None] != own_slot)
            received = jnp.where(live_mask[:, None, :], received, jnp.zeros_like(received))
            received = jnp.transpose(received.reshape(subs, K, CAP // 64, 64), (0, 2, 1, 3))
            own_block = diag_term(vec_rows, blocks, cols)
            row_blocks = couple(vec_rows, received, p_blocks, p_rows)
            row_blocks = row_blocks + (slot_ids == own_slot).astype(jnp.float32)[:, None, None] * own_block[None]
            coarse_line = jnp.transpose(row_blocks, (1, 0, 2)).reshape(K, subs * K)
            return coarse_line, couple(vec_rows, faces, c_blocks, c_rows)

        lines, crossed = jax.vmap(one_sub)(vec_group, blk_group, col_group, row_group, span_group, pb_group, pr_group, cb_group, cr_group, face_group, slot_ids)
        return lines.reshape(subs * K, subs * K), crossed

    group_matrix, cross_rows = lax.map(one_group, (eigvecs, local_blocks, local_cols, margin_rows, margin_lens, peer_blocks, peer_rowblocks, cross_blocks, cross_rowblocks, across))
    return group_matrix, cross_rows
```

```python
import functools

import jax
import jax.numpy as jnp
from jax import lax
from jax.experimental import pallas as pl
from jax.experimental.pallas import tpu as pltpu
from jax.sharding import PartitionSpec as P

K = 48
BND = 512
CAP = 256
FACE = 128
LANES = 128
HALF = 64
MESH = pl.DeviceIdType.MESH
F32 = jnp.float32
BF16 = jnp.bfloat16


def dot_t(a, b):
    return lax.dot_general(a, b, (((1,), (1,)), ((), ())), preferred_element_type=F32)


def dot(a, b):
    return lax.dot_general(a, b, (((1,), (0,)), ((), ())), preferred_element_type=F32)


def kernel(
    subs,
    grps,
    z_hbm,
    lb_hbm,
    pb_hbm,
    cb_hbm,
    cols_hbm,
    rows_hbm,
    lens_hbm,
    prow_hbm,
    crow_hbm,
    out_ref,
    cross_ref,
    cols,
    rows_ref,
    lens,
    prow,
    crow,
    z_v,
    lb_v,
    pb_v,
    cb_v,
    zf,
    zi,
    lf,
    pf,
    cf,
    zz,
    zd,
    zpair,
    take_s,
    take_r,
    mix_s,
    mix_r,
    face,
    a_all,
    d_all,
    got,
    gath,
    in_sem,
    lb_sem,
    ts_sem,
    tr_sem,
    ls_sem,
    lr_sem,
    fs_sem,
    fr_sem,
    rs_sem,
    rr_sem,
):
    me = lax.axis_index("sub")
    g = lax.axis_index("grp")
    nblk = z_v.shape[0]
    nnz = lb_v.shape[0]
    pairs = nblk // 2
    step = nblk + 8
    ncb = CAP // 64
    nfb = FACE // 64

    barrier = pltpu.get_barrier_semaphore()
    for d in range(1, subs):
        pl.semaphore_signal(
            barrier, inc=1, device_id={"sub": lax.rem(me + d, subs)}, device_id_type=MESH
        )

    @pl.when(g > 0)
    def _():
        pl.semaphore_signal(barrier, inc=1, device_id={"grp": g - 1}, device_id_type=MESH)

    @pl.when(g < grps - 1)
    def _():
        pl.semaphore_signal(barrier, inc=1, device_id={"grp": g + 1}, device_id_type=MESH)

    z_in = pltpu.make_async_copy(z_hbm, z_v, in_sem.at[0])
    z_in.start()
    pb_in = pltpu.make_async_copy(pb_hbm, pb_v, in_sem.at[1])
    pb_in.start()
    cb_in = pltpu.make_async_copy(cb_hbm, cb_v, in_sem.at[2])
    cb_in.start()
    small_in = [
        pltpu.make_async_copy(a, b, in_sem.at[3 + i])
        for i, (a, b) in enumerate(
            [
                (prow_hbm, prow),
                (lens_hbm, lens),
                (rows_hbm, rows_ref),
                (cols_hbm, cols),
                (crow_hbm, crow),
            ]
        )
    ]
    for c in small_in:
        c.start()
    lb_in = [pltpu.make_async_copy(lb_hbm.at[t], lb_v.at[t], lb_sem.at[t]) for t in range(nnz)]
    for t in range(nnz):
        lb_in[t].start()

    lane = lax.broadcasted_iota(jnp.int32, (1, LANES), 1)
    lo = lane < HALF

    z_in.wait()
    for q in range(K // 2):
        zf[q * nblk : (q + 1) * nblk, :] = z_v[:, q * LANES : (q + 1) * LANES].astype(F32)

    def z_body(i, carry):
        for s in range(2):
            r = i * 2 + s
            v = zf[pl.ds(r, K // 2, stride=nblk), :]
            w = pltpu.roll(v, HALF, 1)
            zi[pl.ds(r * K, K // 2, stride=2), :] = jnp.where(lo, v, w)
            zi[pl.ds(r * K + 1, K // 2, stride=2), :] = jnp.where(lo, w, v)
        a = zi[pl.ds(i * 2 * K, K), :]
        b = zi[pl.ds(i * 2 * K + K, K), :]
        zz[i * 2] = a.astype(BF16)
        zz[i * 2 + 1] = b.astype(BF16)
        zpair[i] = jnp.where(lo, a, b).astype(BF16)
        return carry

    lax.fori_loop(0, pairs, z_body, 0, unroll=4)

    src = lax.broadcasted_iota(jnp.int32, (LANES, LANES), 0)
    dst = lax.broadcasted_iota(jnp.int32, (LANES, LANES), 1) % HALF
    want = jnp.where(dst < 32, dst * 2, (dst - 32) * 2 + 1)
    sel = jnp.where(src == want, 1.0, 0.0).astype(BF16)

    def d_body(i, carry):
        both = jnp.concatenate([zz[i * 2], zz[i * 2 + 1]], axis=0)
        moved = dot(both, sel)
        a, b = moved[:K], moved[K:]
        zd[i * 2] = a.astype(BF16)
        zd[i * 2 + 1] = b.astype(BF16)
        d_all[:, pl.ds(pl.multiple_of(i * LANES, LANES), LANES)] = jnp.where(lo, a, b).astype(BF16)
        return carry

    lax.fori_loop(0, pairs, d_body, 0, unroll=8)

    pb_in.wait()
    cb_in.wait()
    for c in small_in:
        c.wait()

    def unfold(x0, x1):
        e = jnp.where(lo, x0, pltpu.roll(x1, HALF, 1))
        o = jnp.where(lo, pltpu.roll(x0, HALF, 1), x1)
        return jnp.concatenate([e, o], axis=0).astype(BF16)

    def mix(x0, x1, r0, r1):
        both = jnp.concatenate([zd[r0], zd[r1]], axis=0)[:, :HALF]
        m = dot(both, unfold(x0, x1))
        return jnp.where(lo, m[:K], m[K:]).astype(BF16)

    def p_body(p, carry):
        for m in range(32):
            pf[m * 8 : m * 8 + ncb, :] = pb_v[p, :, m * LANES : (m + 1) * LANES].astype(F32)
        parts = []
        for c in range(0, ncb, 2):
            x0 = pf[pl.ds(c, 32, stride=8), :]
            x1 = pf[pl.ds(c + 1, 32, stride=8), :]
            parts.append(mix(x0, x1, prow[p, c], prow[p, c + 1]))
        mixed = jnp.concatenate(parts, axis=1)
        slots = lax.broadcasted_iota(jnp.int32, (1, CAP), 1)
        limit = jnp.where(p == me, 0, lens[0, p])
        take_s[p] = jnp.where(slots < limit, rows_ref[pl.ds(p, 1), :], -1)
        mix_s[p] = mixed
        return carry

    lax.fori_loop(0, subs, p_body, 0)
    take_r[me] = jnp.full((1, CAP), -1, jnp.int32)
    mix_r[me] = jnp.zeros((K, CAP), BF16)

    waits = subs - 1 + (g > 0).astype(jnp.int32) + (g < grps - 1).astype(jnp.int32)
    pl.semaphore_wait(barrier, waits)

    def take_copy(mine, theirs, peer):
        return pltpu.make_async_remote_copy(
            src_ref=take_s.at[mine],
            dst_ref=take_r.at[theirs],
            send_sem=ts_sem.at[mine],
            recv_sem=tr_sem.at[theirs],
            device_id={"sub": peer},
            device_id_type=MESH,
        )

    def mix_copy(mine, theirs, peer):
        return pltpu.make_async_remote_copy(
            src_ref=mix_s.at[mine],
            dst_ref=mix_r.at[theirs],
            send_sem=ls_sem.at[mine],
            recv_sem=lr_sem.at[theirs],
            device_id={"sub": peer},
            device_id_type=MESH,
        )

    peers = [lax.rem(me + d, subs) for d in range(1, subs)]
    for peer in peers:
        take_copy(peer, me, peer).start()
    for peer in peers:
        mix_copy(peer, me, peer).start()

    def face_copy(side, target):
        return pltpu.make_async_remote_copy(
            src_ref=zpair.at[BND // LANES + 1 - side],
            dst_ref=face.at[side],
            send_sem=fs_sem.at[side],
            recv_sem=fr_sem.at[side],
            device_id={"grp": target},
            device_id_type=MESH,
        )

    @pl.when(g < grps - 1)
    def _():
        face_copy(0, g + 1).start()

    @pl.when(g > 0)
    def _():
        face_copy(1, g - 1).start()


    for t in range(nnz):
        lb_in[t].wait()

    def l_body(t, carry):
        for m in range(32):
            lf[pl.ds((t * 32 + m) * step, nblk), :] = lb_v[
                t, :, m * LANES : (m + 1) * LANES
            ].astype(F32)
        return carry

    lax.fori_loop(0, nnz, l_body, 0)

    zero = jnp.zeros((32, LANES), F32)

    def own_part(r):
        weights, moving = [], []
        for t in range(0, nnz, 2):
            x0 = lf[pl.ds(t * 32 * step + r, 32, stride=step), :]
            if t + 1 < nnz:
                x1 = lf[pl.ds((t + 1) * 32 * step + r, 32, stride=step), :]
                vec = jnp.where(lo, zz[cols[t, 0, r]], zz[cols[t + 1, 0, r]])
            else:
                x1 = zero
                vec = zz[cols[t, 0, r]]
            weights.append(unfold(x0, x1))
            moving.append(vec)
        return dot_t(jnp.concatenate(moving, axis=1), jnp.concatenate(weights, axis=1))

    def r_body(i, carry):
        a = own_part(i * 2)
        b = own_part(i * 2 + 1)
        a_all[:, pl.ds(pl.multiple_of(i * LANES, LANES), LANES)] = jnp.concatenate(
            [a, b], axis=1
        ).astype(BF16)
        return carry

    lax.fori_loop(0, pairs, r_body, 0, unroll=8)
    own = dot_t(a_all[...], d_all[...])

    layer = jnp.concatenate([zpair[h] for h in range(BND // LANES)], axis=1)
    for peer in peers:
        take_copy(peer, peer, peer).wait_recv()

    def g_body(p, carry):
        cells = lax.broadcasted_iota(jnp.int32, (BND, CAP), 0)
        hot = jnp.where(cells == take_r[p], 1.0, 0.0).astype(BF16)
        got[p] = dot(layer, hot).astype(BF16)
        return carry

    lax.fori_loop(0, subs, g_body, 0)

    for peer in peers:
        mix_copy(peer, peer, peer).wait_recv()
    blocks = []
    for p in range(subs):
        blocks.append(dot_t(got[p], mix_r[p]) + jnp.where(p == me, 1.0, 0.0) * own)
    gath[me] = jnp.concatenate(blocks, axis=1).astype(BF16)

    def row_copy(slot, peer):
        return pltpu.make_async_remote_copy(
            src_ref=gath.at[slot],
            dst_ref=gath.at[slot],
            send_sem=rs_sem.at[peer],
            recv_sem=rr_sem.at[slot],
            device_id={"sub": peer},
            device_id_type=MESH,
        )

    for peer in peers:
        row_copy(me, peer).start()

    @pl.when(g > 0)
    def _():
        face_copy(0, g + 1).wait_recv()

    @pl.when(g == 0)
    def _():
        face[0] = jnp.zeros((K, LANES), BF16)

    @pl.when(g < grps - 1)
    def _():
        face_copy(1, g - 1).wait_recv()

    @pl.when(g == grps - 1)
    def _():
        face[1] = jnp.zeros((K, LANES), BF16)

    for q in range(2):
        for m in range(32):
            cf[q * 256 + m * 8 : q * 256 + m * 8 + nfb, :] = cb_v[
                q, :, m * LANES : (m + 1) * LANES
            ].astype(F32)
        x0 = cf[pl.ds(q * 256, 32, stride=8), :]
        x1 = cf[pl.ds(q * 256 + 1, 32, stride=8), :]
        mixed = mix(x0, x1, crow[q, 0], crow[q, 1])
        cross_ref[q] = dot_t(mixed, face[q])

    @pl.when(g < grps - 1)
    def _():
        face_copy(0, g + 1).wait_send()

    @pl.when(g > 0)
    def _():
        face_copy(1, g - 1).wait_send()

    for peer in peers:
        take_copy(peer, me, peer).wait_send()
        mix_copy(peer, me, peer).wait_send()
    for peer in peers:
        row_copy(peer, peer).wait_recv()
    side = subs * K
    unit = jnp.where(
        lax.broadcasted_iota(jnp.int32, (side, side), 0)
        == lax.broadcasted_iota(jnp.int32, (side, side), 1),
        1.0,
        0.0,
    ).astype(BF16)
    out_ref[...] = dot_t(unit, jnp.concatenate([gath[p] for p in range(subs)], axis=0))
    for peer in peers:
        row_copy(me, peer).wait_send()


def emit(matrix, crossed, matrix_hbm, crossed_hbm, sem):
    copies = [
        pltpu.make_async_copy(matrix, matrix_hbm, sem.at[0]),
        pltpu.make_async_copy(crossed, crossed_hbm, sem.at[1]),
    ]
    for c in copies:
        c.start()
    for c in copies:
        c.wait()


def per_device(
    eigvecs,
    local_blocks,
    local_cols,
    margin_rows,
    margin_lens,
    peer_blocks,
    peer_rowblocks,
    cross_blocks,
    cross_rowblocks,
):
    subs = lax.axis_size("sub")
    grps = lax.axis_size("grp")
    z = eigvecs[0, 0]
    lb = jnp.transpose(local_blocks[0, 0], (1, 0, 2))
    cols = jnp.transpose(local_cols[0], (2, 0, 1))
    nblk = z.shape[0]
    nnz = lb.shape[0]
    pb = peer_blocks[0, 0]
    cb = cross_blocks[0, 0]
    vmem = pl.BlockSpec(memory_space=pltpu.VMEM)
    hbm = pl.BlockSpec(memory_space=pltpu.HBM)
    dma = pltpu.SemaphoreType.DMA
    group_matrix, crossed = pl.pallas_call(
        functools.partial(kernel, subs, grps),
        out_shape=(
            pltpu.VMEM((subs * K, subs * K), F32),
            pltpu.VMEM((2, K, K), F32),
        ),
        in_specs=[hbm] * 9,
        out_specs=(vmem, vmem),
        scratch_shapes=[
            pltpu.SMEM(cols.shape, jnp.int32),
            pltpu.VMEM(margin_rows.shape[2:], jnp.int32),
            pltpu.SMEM((1, subs), jnp.int32),
            pltpu.SMEM(peer_rowblocks.shape[2:], jnp.int32),
            pltpu.SMEM(cross_rowblocks.shape[2:], jnp.int32),
            pltpu.VMEM(z.shape, BF16),
            pltpu.VMEM(lb.shape, BF16),
            pltpu.VMEM(pb.shape, BF16),
            pltpu.VMEM(cb.shape, BF16),
            pltpu.VMEM((K // 2 * nblk, LANES), F32),
            pltpu.VMEM((nblk * K, LANES), F32),
            pltpu.VMEM((nnz * 32 * (nblk + 8), LANES), F32),
            pltpu.VMEM((256, LANES), F32),
            pltpu.VMEM((512, LANES), F32),
            pltpu.VMEM((nblk, K, LANES), BF16),
            pltpu.VMEM((nblk, K, LANES), BF16),
            pltpu.VMEM((nblk // 2, K, LANES), BF16),
            pltpu.VMEM((subs, 1, CAP), jnp.int32),
            pltpu.VMEM((subs, 1, CAP), jnp.int32),
            pltpu.VMEM((subs, K, CAP), BF16),
            pltpu.VMEM((subs, K, CAP), BF16),
            pltpu.VMEM((2, K, LANES), BF16),
            pltpu.VMEM((K, nblk * HALF), BF16),
            pltpu.VMEM((K, nblk * HALF), BF16),
            pltpu.VMEM((subs, K, CAP), BF16),
            pltpu.VMEM((subs, K, subs * K), BF16),
            dma((8,)),
            dma((nnz,)),
            dma((subs,)),
            dma((subs,)),
            dma((subs,)),
            dma((subs,)),
            dma((2,)),
            dma((2,)),
            dma((subs,)),
            dma((subs,)),
        ],
        compiler_params=pltpu.CompilerParams(
            collective_id=0, has_side_effects=True, vmem_limit_bytes=40 * 1024 * 1024
        ),
    )(
        *[
            pltpu.with_memory_space_constraint(x, pltpu.HBM)
            for x in (
                z,
                lb,
                pb,
                cb,
                cols,
                margin_rows[0, 0],
                margin_lens[0],
                peer_rowblocks[0, 0],
                cross_rowblocks[0, 0],
            )
        ]
    )
    group_matrix, crossed = pl.pallas_call(
        emit,
        out_shape=(
            jax.ShapeDtypeStruct(group_matrix.shape, F32),
            jax.ShapeDtypeStruct(crossed.shape, F32),
        ),
        in_specs=[vmem, vmem],
        out_specs=(hbm, hbm),
        scratch_shapes=[dma((2,))],
        compiler_params=pltpu.CompilerParams(vmem_limit_bytes=1024 * 1024),
    )(*[pltpu.with_memory_space_constraint(x, pltpu.VMEM) for x in (group_matrix, crossed)])
    return group_matrix[None], crossed[None, None]


def solution(mesh):
    return jax.shard_map(
        per_device,
        mesh=mesh,
        in_specs=(
            P("grp", "sub", None, None),
            P("grp", "sub", None, None, None),
            P("grp", "sub", None, None),
            P("grp", "sub", None, None),
            P("grp", "sub", None),
            P("grp", "sub", None, None, None),
            P("grp", "sub", None, None),
            P("grp", "sub", None, None, None),
            P("grp", "sub", None, None),
        ),
        out_specs=(P("grp", None, None), P("grp", "sub", None, None, None)),
        check_vma=False,
    )
```

```python
import functools

import jax
import jax.numpy as jnp
from jax import lax
from jax.experimental import pallas as pl
from jax.experimental.pallas import tpu as pltpu
from jax.sharding import PartitionSpec as P

K = 48
BND = 512
CAP = 256
FACE = 128
LANES = 128
HALF = 64
MESH = pl.DeviceIdType.MESH
F32 = jnp.float32
BF16 = jnp.bfloat16


def dot_t(a, b):
    return lax.dot_general(a, b, (((1,), (1,)), ((), ())), preferred_element_type=F32)


def dot(a, b):
    return lax.dot_general(a, b, (((1,), (0,)), ((), ())), preferred_element_type=F32)


def kernel(
    subs,
    grps,
    z_hbm,
    lb_hbm,
    pb_hbm,
    cb_hbm,
    cols_hbm,
    rows_hbm,
    lens_hbm,
    prow_hbm,
    crow_hbm,
    out_ref,
    cross_ref,
    cols,
    rows_ref,
    lens,
    prow,
    crow,
    z_v,
    lb_v,
    pb_v,
    cb_v,
    zf,
    zi,
    lf,
    pf,
    cf,
    zz,
    zpair,
    take_s,
    take_r,
    mix_s,
    mix_r,
    face,
    a_all,
    d_all,
    got,
    gath,
    take_x,
    mix_x,
    layer_x,
    diag_s,
    diag_r,
    in_sem,
    lb_sem,
    ts_sem,
    tr_sem,
    ls_sem,
    lr_sem,
    fs_sem,
    fr_sem,
    rs_sem,
    rr_sem,
    xt_sem,
    xm_sem,
    one_sem,
):
    me = lax.axis_index("sub")
    g = lax.axis_index("grp")
    nblk = z_v.shape[0]
    nnz = lb_v.shape[0]
    pairs = nblk // 2
    step = nblk + 8
    ncb = CAP // 64
    nfb = FACE // 64
    last = subs - 1
    peers = [lax.rem(me + d, subs) for d in range(subs - 1, 0, -1)]
    sides = (g > 0).astype(jnp.int32) + (g < grps - 1).astype(jnp.int32)
    waits = last + sides
    lead = g == 0

    z_in = pltpu.make_async_copy(z_hbm, z_v, in_sem.at[0])
    z_in.start()
    barrier = pltpu.get_barrier_semaphore()
    below = g > 0
    above = g < grps - 1
    for peer in peers:
        pl.semaphore_signal(barrier, inc=1, device_id={"sub": peer}, device_id_type=MESH)

    @pl.when(below)
    def _():
        pl.semaphore_signal(barrier, inc=1, device_id={"grp": g - 1}, device_id_type=MESH)

    @pl.when(above)
    def _():
        pl.semaphore_signal(barrier, inc=1, device_id={"grp": g + 1}, device_id_type=MESH)

    pb_in = pltpu.make_async_copy(pb_hbm, pb_v, in_sem.at[1])
    pb_in.start()
    cb_in = pltpu.make_async_copy(cb_hbm, cb_v, in_sem.at[2])
    cb_in.start()
    small_in = [
        pltpu.make_async_copy(a, b, in_sem.at[3 + i])
        for i, (a, b) in enumerate(
            [
                (prow_hbm, prow),
                (lens_hbm, lens),
                (rows_hbm, rows_ref),
                (cols_hbm, cols),
                (crow_hbm, crow),
            ]
        )
    ]
    for c in small_in:
        c.start()
    lb_in = [pltpu.make_async_copy(lb_hbm.at[t], lb_v.at[t], lb_sem.at[t]) for t in range(nnz)]
    for t in range(nnz):
        lb_in[t].start()

    lane = lax.broadcasted_iota(jnp.int32, (1, LANES), 1)
    lo = lane < HALF

    z_in.wait()
    for q in range(K // 2):
        zf[q * nblk : (q + 1) * nblk, :] = z_v[:, q * LANES : (q + 1) * LANES].astype(F32)

    def z_body(i, carry):
        for s in range(2):
            r = i * 2 + s
            v = zf[pl.ds(r, K // 2, stride=nblk), :]
            w = pltpu.roll(v, HALF, 1)
            zi[pl.ds(r * K, K // 2, stride=2), :] = jnp.where(lo, v, w)
            zi[pl.ds(r * K + 1, K // 2, stride=2), :] = jnp.where(lo, w, v)
        a = zi[pl.ds(i * 2 * K, K), :]
        b = zi[pl.ds(i * 2 * K + K, K), :]
        zz[i * 2] = a.astype(BF16)
        zz[i * 2 + 1] = b.astype(BF16)
        zpair[i] = jnp.where(lo, a, b).astype(BF16)
        return carry

    lax.fori_loop(0, pairs, z_body, 0, unroll=4)

    src = lax.broadcasted_iota(jnp.int32, (LANES, LANES), 0)
    dst = lax.broadcasted_iota(jnp.int32, (LANES, LANES), 1) % HALF
    want = jnp.where(dst < 32, dst * 2, (dst - 32) * 2 + 1)
    sel = jnp.where(src == want, 1.0, 0.0).astype(BF16)

    def take_copy(mine, theirs, peer):
        return pltpu.make_async_remote_copy(
            src_ref=take_s.at[mine],
            dst_ref=take_r.at[theirs],
            send_sem=ts_sem.at[mine],
            recv_sem=tr_sem.at[theirs],
            device_id={"sub": peer},
            device_id_type=MESH,
        )

    def mix_copy(mine, theirs, peer):
        return pltpu.make_async_remote_copy(
            src_ref=mix_s.at[mine],
            dst_ref=mix_r.at[theirs],
            send_sem=ls_sem.at[mine],
            recv_sem=lr_sem.at[theirs],
            device_id={"sub": peer},
            device_id_type=MESH,
        )

    def extra_take(slot):
        return pltpu.make_async_remote_copy(
            src_ref=take_s.at[last],
            dst_ref=take_x.at[slot],
            send_sem=one_sem.at[0],
            recv_sem=xt_sem.at[slot],
            device_id={"sub": 0},
            device_id_type=MESH,
        )

    def extra_mix(slot):
        return pltpu.make_async_remote_copy(
            src_ref=mix_s.at[last],
            dst_ref=mix_x.at[slot],
            send_sem=one_sem.at[1],
            recv_sem=xm_sem.at[slot],
            device_id={"sub": 0},
            device_id_type=MESH,
        )

    def layer_copy():
        return pltpu.make_async_remote_copy(
            src_ref=zpair.at[pl.ds(0, BND // LANES)],
            dst_ref=layer_x,
            send_sem=one_sem.at[2],
            recv_sem=one_sem.at[3],
            device_id={"sub": 0},
            device_id_type=MESH,
        )

    def diag_copy():
        return pltpu.make_async_remote_copy(
            src_ref=diag_s,
            dst_ref=diag_r,
            send_sem=one_sem.at[4],
            recv_sem=one_sem.at[5],
            device_id={"sub": 0},
            device_id_type=MESH,
        )

    for c in small_in:
        c.wait()
    slots = lax.broadcasted_iota(jnp.int32, (1, CAP), 1)
    for peer in peers:
        take_s[peer] = jnp.where(slots < lens[0, peer], rows_ref[pl.ds(peer, 1), :], -1)
    mix_r[me] = jnp.zeros((K, CAP), BF16)

    @pl.when(me == last)
    def _():
        pl.semaphore_wait(barrier, waits)

        for p in range(last):
            take_copy(p, last, p).start()

    pb_in.wait()

    def unfold(x0, x1):
        e = jnp.where(lo, x0, pltpu.roll(x1, HALF, 1))
        o = jnp.where(lo, pltpu.roll(x0, HALF, 1), x1)
        return jnp.concatenate([e, o], axis=0).astype(BF16)

    def mix(x0, x1, r0, r1):
        both = dot(jnp.concatenate([zz[r0], zz[r1]], axis=0), sel).astype(BF16)[:, :HALF]
        m = dot(both, unfold(x0, x1))
        return jnp.where(lo, m[:K], m[K:]).astype(BF16)

    for n, peer in enumerate(peers):
        for m in range(32):
            pf[n * 256 + m * 8 : n * 256 + m * 8 + ncb, :] = pb_v[
                peer, :, m * LANES : (m + 1) * LANES
            ].astype(F32)
    for n, peer in enumerate(peers):
        for c in range(0, ncb, 2):
            x0 = pf[pl.ds(n * 256 + c, 32, stride=8), :]
            x1 = pf[pl.ds(n * 256 + c + 1, 32, stride=8), :]
            mix_s[peer, :, c * HALF : (c + 2) * HALF] = mix(
                x0, x1, prow[peer, c], prow[peer, c + 1]
            )

    @pl.when(me == last)
    def _():
        for p in [*range(1, last), 0]:
            mix_copy(p, last, p).start()

        @pl.when(lead)
        def _():
            layer_copy().start()

    @pl.when(me != last)
    def _():
        pl.semaphore_wait(barrier, waits)
        sends = [last, *range(1, last), 0]
        between = jnp.logical_and(lead, me > 0)

        @pl.when(between)
        def _():
            extra_take(me).start()

        for copy in (take_copy, mix_copy):
            for p in sends:

                @pl.when(p != me)
                def _():
                    copy(p, me, p).start()

        @pl.when(between)
        def _():
            extra_mix(me).start()

    def face_copy(side, target):
        return pltpu.make_async_remote_copy(
            src_ref=zpair.at[BND // LANES + 1 - side],
            dst_ref=face.at[side],
            send_sem=fs_sem.at[side],
            recv_sem=fr_sem.at[side],
            device_id={"grp": target},
            device_id_type=MESH,
        )

    @pl.when(above)
    def _():
        face_copy(0, g + 1).start()

    @pl.when(below)
    def _():
        face_copy(1, g - 1).start()


    def d_body(i, carry):
        both = jnp.concatenate([zz[i * 2], zz[i * 2 + 1]], axis=0)
        moved = dot(both, sel)
        a, b = moved[:K], moved[K:]
        d_all[:, pl.ds(pl.multiple_of(i * LANES, LANES), LANES)] = jnp.where(lo, a, b).astype(BF16)
        return carry

    lax.fori_loop(0, pairs, d_body, 0, unroll=8)

    for t in range(nnz):
        lb_in[t].wait()

    def l_body(t, carry):
        for m in range(32):
            lf[pl.ds((t * 32 + m) * step, nblk), :] = lb_v[
                t, :, m * LANES : (m + 1) * LANES
            ].astype(F32)
        return carry

    lax.fori_loop(0, nnz, l_body, 0)

    zero = jnp.zeros((32, LANES), F32)

    def own_part(r):
        weights, moving = [], []
        for t in range(0, nnz, 2):
            x0 = lf[pl.ds(t * 32 * step + r, 32, stride=step), :]
            if t + 1 < nnz:
                x1 = lf[pl.ds((t + 1) * 32 * step + r, 32, stride=step), :]
                vec = jnp.where(lo, zz[cols[t, 0, r]], zz[cols[t + 1, 0, r]])
            else:
                x1 = zero
                vec = zz[cols[t, 0, r]]
            weights.append(unfold(x0, x1))
            moving.append(vec)
        return dot_t(jnp.concatenate(moving, axis=1), jnp.concatenate(weights, axis=1))

    def r_body(i, carry):
        a = own_part(i * 2)
        b = own_part(i * 2 + 1)
        a_all[:, pl.ds(pl.multiple_of(i * LANES, LANES), LANES)] = jnp.concatenate(
            [a, b], axis=1
        ).astype(BF16)
        return carry

    lax.fori_loop(0, pairs, r_body, 0, unroll=16)
    own = dot_t(a_all[...], d_all[...])

    def picked(cells_of, take):
        cells = lax.broadcasted_iota(jnp.int32, (BND, CAP), 0)
        hot = jnp.where(cells == take, 1.0, 0.0).astype(BF16)
        return dot(cells_of, hot).astype(BF16)

    @pl.when(jnp.logical_and(lead, me == last))
    def _():
        diag_s[...] = own.astype(BF16)
        diag_copy().start()

    layer = jnp.concatenate([zpair[h] for h in range(BND // LANES)], axis=1)
    got[me] = jnp.zeros((K, CAP), BF16)

    def row_copy(slot, peer):
        return pltpu.make_async_remote_copy(
            src_ref=gath.at[slot],
            dst_ref=gath.at[slot],
            send_sem=rs_sem.at[peer],
            recv_sem=rr_sem.at[slot],
            device_id={"sub": peer},
            device_id_type=MESH,
        )

    for p in [*range(1, last), 0, last]:
        @pl.when(p != me)
        def _():
            take_copy(p, p, p).wait_recv()
            got[p] = picked(layer, take_r[p])
            mix_copy(p, p, p).wait_recv()

        block = dot_t(got[p], mix_r[p]) + jnp.where(p == me, 1.0, 0.0) * own
        gath[me, :, p * K : (p + 1) * K] = block.astype(BF16)

    for p in range(subs):
        direct = p != me
        if p == 0:
            direct = jnp.logical_and(direct, jnp.logical_not(jnp.logical_and(lead, me == last)))

        @pl.when(direct)
        def _():
            row_copy(me, p).start()

    @pl.when(g > 0)
    def _():
        face_copy(0, g + 1).wait_recv()

    @pl.when(g == 0)
    def _():
        face[0] = jnp.zeros((K, LANES), BF16)

    @pl.when(g < grps - 1)
    def _():
        face_copy(1, g - 1).wait_recv()

    @pl.when(g == grps - 1)
    def _():
        face[1] = jnp.zeros((K, LANES), BF16)

    cb_in.wait()
    for q in range(2):
        for m in range(32):
            cf[q * 256 + m * 8 : q * 256 + m * 8 + nfb, :] = cb_v[
                q, :, m * LANES : (m + 1) * LANES
            ].astype(F32)
        x0 = cf[pl.ds(q * 256, 32, stride=8), :]
        x1 = cf[pl.ds(q * 256 + 1, 32, stride=8), :]
        mixed = mix(x0, x1, crow[q, 0], crow[q, 1])
        cross_ref[q] = dot_t(mixed, face[q])

    @pl.when(g < grps - 1)
    def _():
        face_copy(0, g + 1).wait_send()

    @pl.when(g > 0)
    def _():
        face_copy(1, g - 1).wait_send()

    for peer in peers:
        take_copy(peer, me, peer).wait_send()
        mix_copy(peer, me, peer).wait_send()

    side = subs * K
    unit = jnp.where(
        lax.broadcasted_iota(jnp.int32, (side, side), 0)
        == lax.broadcasted_iota(jnp.int32, (side, side), 1),
        1.0,
        0.0,
    ).astype(BF16)

    def put(p):
        out_ref[:, p * K : (p + 1) * K] = dot_t(unit, gath[p])

    @pl.when(jnp.logical_and(lead, me == 0))
    def _():
        layer_copy().wait_recv()
        theirs = jnp.concatenate([layer_x[h] for h in range(BND // LANES)], axis=1)
        for p in range(1, last):
            extra_take(p).wait_recv()
            extra_mix(p).wait_recv()
        for p in range(last):
            take, mixed = (take_x[p], mix_x[p]) if p else (take_s[last], mix_s[last])
            block = dot_t(picked(theirs, take), mixed)
            gath[last, :, p * K : (p + 1) * K] = block.astype(BF16)
        diag_copy().wait_recv()
        gath[last, :, last * K :] = diag_r[...]
        put(0)
        put(last)
        for p in range(1, last):
            row_copy(p, p).wait_recv()
            put(p)

    @pl.when(jnp.logical_not(jnp.logical_and(lead, me == 0)))
    def _():
        for p in range(subs):

            @pl.when(p != me)
            def _():
                row_copy(p, p).wait_recv()

        out_ref[...] = dot_t(unit, jnp.concatenate([gath[p] for p in range(subs)], axis=0))

    @pl.when(jnp.logical_and(lead, me == last))
    def _():
        layer_copy().wait_send()
        diag_copy().wait_send()

    @pl.when(jnp.logical_and(lead, jnp.logical_and(me > 0, me < last)))
    def _():
        extra_take(me).wait_send()
        extra_mix(me).wait_send()

    for p in range(subs):
        direct = p != me
        if p == 0:
            direct = jnp.logical_and(direct, jnp.logical_not(jnp.logical_and(lead, me == last)))

        @pl.when(direct)
        def _():
            row_copy(me, p).wait_send()


def emit(matrix, crossed, matrix_hbm, crossed_hbm, sem):
    copies = [
        pltpu.make_async_copy(matrix, matrix_hbm, sem.at[0]),
        pltpu.make_async_copy(crossed, crossed_hbm, sem.at[1]),
    ]
    for c in copies:
        c.start()
    for c in copies:
        c.wait()


def per_device(
    eigvecs,
    local_blocks,
    local_cols,
    margin_rows,
    margin_lens,
    peer_blocks,
    peer_rowblocks,
    cross_blocks,
    cross_rowblocks,
):
    subs = lax.axis_size("sub")
    grps = lax.axis_size("grp")
    z = eigvecs[0, 0]
    lb = jnp.transpose(local_blocks[0, 0], (1, 0, 2))
    cols = jnp.transpose(local_cols[0], (2, 0, 1))
    nblk = z.shape[0]
    nnz = lb.shape[0]
    pb = peer_blocks[0, 0]
    cb = cross_blocks[0, 0]
    vmem = pl.BlockSpec(memory_space=pltpu.VMEM)
    hbm = pl.BlockSpec(memory_space=pltpu.HBM)
    dma = pltpu.SemaphoreType.DMA
    group_matrix, crossed = pl.pallas_call(
        functools.partial(kernel, subs, grps),
        out_shape=(
            pltpu.VMEM((subs * K, subs * K), F32),
            pltpu.VMEM((2, K, K), F32),
        ),
        in_specs=[hbm] * 9,
        out_specs=(vmem, vmem),
        scratch_shapes=[
            pltpu.SMEM(cols.shape, jnp.int32),
            pltpu.VMEM(margin_rows.shape[2:], jnp.int32),
            pltpu.SMEM((1, subs), jnp.int32),
            pltpu.SMEM(peer_rowblocks.shape[2:], jnp.int32),
            pltpu.SMEM(cross_rowblocks.shape[2:], jnp.int32),
            pltpu.VMEM(z.shape, BF16),
            pltpu.VMEM(lb.shape, BF16),
            pltpu.VMEM(pb.shape, BF16),
            pltpu.VMEM(cb.shape, BF16),
            pltpu.VMEM((K // 2 * nblk, LANES), F32),
            pltpu.VMEM((nblk * K, LANES), F32),
            pltpu.VMEM((nnz * 32 * (nblk + 8), LANES), F32),
            pltpu.VMEM(((subs - 1) * 256, LANES), F32),
            pltpu.VMEM((512, LANES), F32),
            pltpu.VMEM((nblk, K, LANES), BF16),
            pltpu.VMEM((nblk // 2, K, LANES), BF16),
            pltpu.VMEM((subs, 1, CAP), jnp.int32),
            pltpu.VMEM((subs, 1, CAP), jnp.int32),
            pltpu.VMEM((subs, K, CAP), BF16),
            pltpu.VMEM((subs, K, CAP), BF16),
            pltpu.VMEM((2, K, LANES), BF16),
            pltpu.VMEM((K, nblk * HALF), BF16),
            pltpu.VMEM((K, nblk * HALF), BF16),
            pltpu.VMEM((subs, K, CAP), BF16),
            pltpu.VMEM((subs, K, subs * K), BF16),
            pltpu.VMEM((subs, 1, CAP), jnp.int32),
            pltpu.VMEM((subs, K, CAP), BF16),
            pltpu.VMEM((BND // LANES, K, LANES), BF16),
            pltpu.VMEM((K, K), BF16),
            pltpu.VMEM((K, K), BF16),
            dma((8,)),
            dma((nnz,)),
            dma((subs,)),
            dma((subs,)),
            dma((subs,)),
            dma((subs,)),
            dma((2,)),
            dma((2,)),
            dma((subs,)),
            dma((subs,)),
            dma((subs,)),
            dma((subs,)),
            dma((6,)),
        ],
        compiler_params=pltpu.CompilerParams(
            collective_id=0, has_side_effects=True, vmem_limit_bytes=40 * 1024 * 1024
        ),
    )(
        *[
            pltpu.with_memory_space_constraint(x, pltpu.HBM)
            for x in (
                z,
                lb,
                pb,
                cb,
                cols,
                margin_rows[0, 0],
                margin_lens[0],
                peer_rowblocks[0, 0],
                cross_rowblocks[0, 0],
            )
        ]
    )
    group_matrix, crossed = pl.pallas_call(
        emit,
        out_shape=(
            jax.ShapeDtypeStruct(group_matrix.shape, F32),
            jax.ShapeDtypeStruct(crossed.shape, F32),
        ),
        in_specs=[vmem, vmem],
        out_specs=(hbm, hbm),
        scratch_shapes=[dma((2,))],
        compiler_params=pltpu.CompilerParams(vmem_limit_bytes=1024 * 1024),
    )(*[pltpu.with_memory_space_constraint(x, pltpu.VMEM) for x in (group_matrix, crossed)])
    return group_matrix[None], crossed[None, None]


def solution(mesh):
    return jax.shard_map(
        per_device,
        mesh=mesh,
        in_specs=(
            P("grp", "sub", None, None),
            P("grp", "sub", None, None, None),
            P("grp", "sub", None, None),
            P("grp", "sub", None, None),
            P("grp", "sub", None),
            P("grp", "sub", None, None, None),
            P("grp", "sub", None, None),
            P("grp", "sub", None, None, None),
            P("grp", "sub", None, None),
        ),
        out_specs=(P("grp", None, None), P("grp", "sub", None, None, None)),
        check_vma=False,
    )
```

```python
import functools

import jax
import jax.numpy as jnp
from jax import lax
from jax.experimental import pallas as pl
from jax.experimental.pallas import tpu as pltpu
from jax.sharding import PartitionSpec as P

K = 48
BND = 512
CAP = 256
FACE = 128
LANES = 128
HALF = 64
MESH = pl.DeviceIdType.MESH
F32 = jnp.float32
BF16 = jnp.bfloat16


def dot_t(a, b):
    return lax.dot_general(a, b, (((1,), (1,)), ((), ())), preferred_element_type=F32)


def dot(a, b):
    return lax.dot_general(a, b, (((1,), (0,)), ((), ())), preferred_element_type=F32)


def kernel(
    subs,
    grps,
    z_hbm,
    lb_hbm,
    pb_hbm,
    cb_hbm,
    cols_hbm,
    rows_hbm,
    lens_hbm,
    prow_hbm,
    crow_hbm,
    out_ref,
    cross_ref,
    cols,
    rows_ref,
    lens,
    prow,
    crow,
    z_v,
    lb_v,
    pb_v,
    cb_v,
    zf,
    zi,
    lf,
    pf,
    cf,
    zz,
    zpair,
    take_s,
    take_r,
    mix_s,
    mix_r,
    face,
    a_all,
    d_all,
    got,
    gath,
    take_x,
    mix_x,
    layer_x,
    diag_s,
    diag_r,
    in_sem,
    lb_sem,
    ts_sem,
    tr_sem,
    ls_sem,
    lr_sem,
    fs_sem,
    fr_sem,
    rs_sem,
    rr_sem,
    xt_sem,
    xm_sem,
    one_sem,
    ready,
):
    me = lax.axis_index("sub")
    g = lax.axis_index("grp")
    nblk = z_v.shape[0]
    nnz = lb_v.shape[0]
    pairs = nblk // 2
    step = nblk + 8
    ncb = CAP // 64
    nfb = FACE // 64
    last = subs - 1
    peers = [lax.rem(me + d, subs) for d in range(subs - 1, 0, -1)]
    sides = (g > 0).astype(jnp.int32) + (g < grps - 1).astype(jnp.int32)
    lead = g == 0
    first = jnp.logical_and(lead, me == 0)
    waits = last + sides - first.astype(jnp.int32)

    z_in = pltpu.make_async_copy(z_hbm, z_v, in_sem.at[0])
    z_in.start()
    barrier = pltpu.get_barrier_semaphore()
    below = g > 0
    above = g < grps - 1
    for p in range(subs):
        greet = p != me
        if p == 0:
            greet = jnp.logical_and(greet, jnp.logical_not(jnp.logical_and(lead, me == last)))

        @pl.when(greet)
        def _():
            pl.semaphore_signal(barrier, inc=1, device_id={"sub": p}, device_id_type=MESH)

    @pl.when(below)
    def _():
        pl.semaphore_signal(barrier, inc=1, device_id={"grp": g - 1}, device_id_type=MESH)

    @pl.when(above)
    def _():
        pl.semaphore_signal(barrier, inc=1, device_id={"grp": g + 1}, device_id_type=MESH)

    pb_in = pltpu.make_async_copy(pb_hbm, pb_v, in_sem.at[1])
    pb_in.start()
    cb_in = pltpu.make_async_copy(cb_hbm, cb_v, in_sem.at[2])
    cb_in.start()
    small_in = [
        pltpu.make_async_copy(a, b, in_sem.at[3 + i])
        for i, (a, b) in enumerate(
            [
                (prow_hbm, prow),
                (lens_hbm, lens),
                (rows_hbm, rows_ref),
                (cols_hbm, cols),
                (crow_hbm, crow),
            ]
        )
    ]
    for c in small_in:
        c.start()
    lb_in = [pltpu.make_async_copy(lb_hbm.at[t], lb_v.at[t], lb_sem.at[t]) for t in range(nnz)]
    for t in range(nnz):
        lb_in[t].start()

    lane = lax.broadcasted_iota(jnp.int32, (1, LANES), 1)
    lo = lane < HALF

    z_in.wait()
    for q in range(K // 2):
        zf[q * nblk : (q + 1) * nblk, :] = z_v[:, q * LANES : (q + 1) * LANES].astype(F32)

    def z_body(i, carry):
        for s in range(2):
            r = i * 2 + s
            v = zf[pl.ds(r, K // 2, stride=nblk), :]
            w = pltpu.roll(v, HALF, 1)
            zi[pl.ds(r * K, K // 2, stride=2), :] = jnp.where(lo, v, w)
            zi[pl.ds(r * K + 1, K // 2, stride=2), :] = jnp.where(lo, w, v)
        a = zi[pl.ds(i * 2 * K, K), :]
        b = zi[pl.ds(i * 2 * K + K, K), :]
        zz[i * 2] = a.astype(BF16)
        zz[i * 2 + 1] = b.astype(BF16)
        zpair[i] = jnp.where(lo, a, b).astype(BF16)
        return carry

    lax.fori_loop(0, pairs, z_body, 0, unroll=4)

    src = lax.broadcasted_iota(jnp.int32, (LANES, LANES), 0)
    dst = lax.broadcasted_iota(jnp.int32, (LANES, LANES), 1) % HALF
    want = jnp.where(dst < 32, dst * 2, (dst - 32) * 2 + 1)
    sel = jnp.where(src == want, 1.0, 0.0).astype(BF16)

    def take_copy(mine, theirs, peer):
        return pltpu.make_async_remote_copy(
            src_ref=take_s.at[mine],
            dst_ref=take_r.at[theirs],
            send_sem=ts_sem.at[mine],
            recv_sem=tr_sem.at[theirs],
            device_id={"sub": peer},
            device_id_type=MESH,
        )

    def mix_copy(mine, theirs, peer):
        return pltpu.make_async_remote_copy(
            src_ref=mix_s.at[mine],
            dst_ref=mix_r.at[theirs],
            send_sem=ls_sem.at[mine],
            recv_sem=lr_sem.at[theirs],
            device_id={"sub": peer},
            device_id_type=MESH,
        )

    def extra_take(slot):
        return pltpu.make_async_remote_copy(
            src_ref=take_s.at[last],
            dst_ref=take_x.at[slot],
            send_sem=one_sem.at[0],
            recv_sem=xt_sem.at[slot],
            device_id={"sub": 0},
            device_id_type=MESH,
        )

    def extra_mix(slot):
        return pltpu.make_async_remote_copy(
            src_ref=mix_s.at[last],
            dst_ref=mix_x.at[slot],
            send_sem=one_sem.at[1],
            recv_sem=xm_sem.at[slot],
            device_id={"sub": 0},
            device_id_type=MESH,
        )

    def layer_copy():
        return pltpu.make_async_remote_copy(
            src_ref=zpair.at[pl.ds(0, BND // LANES)],
            dst_ref=layer_x,
            send_sem=one_sem.at[2],
            recv_sem=one_sem.at[3],
            device_id={"sub": 0},
            device_id_type=MESH,
        )

    def diag_copy():
        return pltpu.make_async_remote_copy(
            src_ref=diag_s,
            dst_ref=diag_r,
            send_sem=one_sem.at[4],
            recv_sem=one_sem.at[5],
            device_id={"sub": 0},
            device_id_type=MESH,
        )

    for c in small_in:
        c.wait()
    slots = lax.broadcasted_iota(jnp.int32, (1, CAP), 1)
    for peer in peers:
        take_s[peer] = jnp.where(slots < lens[0, peer], rows_ref[pl.ds(peer, 1), :], -1)
    mix_r[me] = jnp.zeros((K, CAP), BF16)

    @pl.when(me == last)
    def _():
        pl.semaphore_wait(barrier, waits)

        @pl.when(lead)
        def _():
            pl.semaphore_signal(ready, inc=1, device_id={"sub": 0}, device_id_type=MESH)

        for p in range(last):
            take_copy(p, last, p).start()

    pb_in.wait()

    def unfold(x0, x1):
        e = jnp.where(lo, x0, pltpu.roll(x1, HALF, 1))
        o = jnp.where(lo, pltpu.roll(x0, HALF, 1), x1)
        return jnp.concatenate([e, o], axis=0).astype(BF16)

    def mix(x0, x1, r0, r1):
        both = dot(jnp.concatenate([zz[r0], zz[r1]], axis=0), sel).astype(BF16)[:, :HALF]
        m = dot(both, unfold(x0, x1))
        return jnp.where(lo, m[:K], m[K:]).astype(BF16)

    for n, peer in enumerate(peers):
        for m in range(32):
            pf[n * 256 + m * 8 : n * 256 + m * 8 + ncb, :] = pb_v[
                peer, :, m * LANES : (m + 1) * LANES
            ].astype(F32)
    for n, peer in enumerate(peers):
        for c in range(0, ncb, 2):
            x0 = pf[pl.ds(n * 256 + c, 32, stride=8), :]
            x1 = pf[pl.ds(n * 256 + c + 1, 32, stride=8), :]
            mix_s[peer, :, c * HALF : (c + 2) * HALF] = mix(
                x0, x1, prow[peer, c], prow[peer, c + 1]
            )

    @pl.when(me == last)
    def _():
        for p in [*range(1, last), 0]:
            mix_copy(p, last, p).start()

        @pl.when(lead)
        def _():
            layer_copy().start()

    @pl.when(me != last)
    def _():
        pl.semaphore_wait(barrier, waits)
        sends = [*range(1, last), last, 0]
        between = jnp.logical_and(lead, me > 0)

        @pl.when(between)
        def _():
            extra_take(me).start()

        for copy in (take_copy, mix_copy):
            for p in sends:

                now = p != me
                if p == last:
                    now = jnp.logical_and(now, jnp.logical_not(first))

                @pl.when(now)
                def _():
                    copy(p, me, p).start()

        @pl.when(between)
        def _():
            extra_mix(me).start()

    def face_copy(side, target):
        return pltpu.make_async_remote_copy(
            src_ref=zpair.at[BND // LANES + 1 - side],
            dst_ref=face.at[side],
            send_sem=fs_sem.at[side],
            recv_sem=fr_sem.at[side],
            device_id={"grp": target},
            device_id_type=MESH,
        )

    @pl.when(above)
    def _():
        face_copy(0, g + 1).start()

    @pl.when(below)
    def _():
        face_copy(1, g - 1).start()


    for t in range(nnz):
        lb_in[t].wait()

    def l_body(t, carry):
        for m in range(32):
            lf[pl.ds((t * 32 + m) * step, nblk), :] = lb_v[
                t, :, m * LANES : (m + 1) * LANES
            ].astype(F32)
        return carry

    lax.fori_loop(0, nnz, l_body, 0)

    zero = jnp.zeros((32, LANES), F32)

    def own_part(r):
        weights, moving = [], []
        for t in range(0, nnz, 2):
            x0 = lf[pl.ds(t * 32 * step + r, 32, stride=step), :]
            if t + 1 < nnz:
                x1 = lf[pl.ds((t + 1) * 32 * step + r, 32, stride=step), :]
                vec = jnp.where(lo, zz[cols[t, 0, r]], zz[cols[t + 1, 0, r]])
            else:
                x1 = zero
                vec = zz[cols[t, 0, r]]
            weights.append(unfold(x0, x1))
            moving.append(vec)
        return dot_t(jnp.concatenate(moving, axis=1), jnp.concatenate(weights, axis=1))

    def r_body(i, carry):
        at = pl.multiple_of(i * LANES, LANES)
        moved = dot(jnp.concatenate([zz[i * 2], zz[i * 2 + 1]], axis=0), sel)
        d_all[:, pl.ds(at, LANES)] = jnp.where(lo, moved[:K], moved[K:]).astype(BF16)
        a = own_part(i * 2)
        b = own_part(i * 2 + 1)
        a_all[:, pl.ds(at, LANES)] = jnp.concatenate(
            [a, b], axis=1
        ).astype(BF16)
        return carry

    lax.fori_loop(0, pairs, r_body, 0, unroll=16)
    own = dot_t(a_all[...], d_all[...])

    def picked(cells_of, take):
        cells = lax.broadcasted_iota(jnp.int32, (BND, CAP), 0)
        hot = jnp.where(cells == take, 1.0, 0.0).astype(BF16)
        return dot(cells_of, hot).astype(BF16)

    @pl.when(jnp.logical_and(lead, me == last))
    def _():
        diag_s[...] = own.astype(BF16)
        diag_copy().start()

    @pl.when(first)
    def _():
        pl.semaphore_wait(ready, 1)
        take_copy(last, 0, last).start()
        mix_copy(last, 0, last).start()

    layer = jnp.concatenate([zpair[h] for h in range(BND // LANES)], axis=1)
    got[me] = jnp.zeros((K, CAP), BF16)

    def row_copy(slot, peer):
        return pltpu.make_async_remote_copy(
            src_ref=gath.at[slot],
            dst_ref=gath.at[slot],
            send_sem=rs_sem.at[peer],
            recv_sem=rr_sem.at[slot],
            device_id={"sub": peer},
            device_id_type=MESH,
        )

    for p in [*range(1, last), 0, last]:
        @pl.when(p != me)
        def _():
            take_copy(p, p, p).wait_recv()
            got[p] = picked(layer, take_r[p])
            mix_copy(p, p, p).wait_recv()

        block = dot_t(got[p], mix_r[p]) + jnp.where(p == me, 1.0, 0.0) * own
        gath[me, :, p * K : (p + 1) * K] = block.astype(BF16)

    for p in range(subs):
        direct = p != me
        if p == 0:
            direct = jnp.logical_and(direct, jnp.logical_not(jnp.logical_and(lead, me == last)))

        @pl.when(direct)
        def _():
            row_copy(me, p).start()

    @pl.when(g > 0)
    def _():
        face_copy(0, g + 1).wait_recv()

    @pl.when(g == 0)
    def _():
        face[0] = jnp.zeros((K, LANES), BF16)

    @pl.when(g < grps - 1)
    def _():
        face_copy(1, g - 1).wait_recv()

    @pl.when(g == grps - 1)
    def _():
        face[1] = jnp.zeros((K, LANES), BF16)

    cb_in.wait()
    for q in range(2):
        for m in range(32):
            cf[q * 256 + m * 8 : q * 256 + m * 8 + nfb, :] = cb_v[
                q, :, m * LANES : (m + 1) * LANES
            ].astype(F32)
        x0 = cf[pl.ds(q * 256, 32, stride=8), :]
        x1 = cf[pl.ds(q * 256 + 1, 32, stride=8), :]
        mixed = mix(x0, x1, crow[q, 0], crow[q, 1])
        cross_ref[q] = dot_t(mixed, face[q])

    @pl.when(g < grps - 1)
    def _():
        face_copy(0, g + 1).wait_send()

    @pl.when(g > 0)
    def _():
        face_copy(1, g - 1).wait_send()

    for peer in peers:
        take_copy(peer, me, peer).wait_send()
        mix_copy(peer, me, peer).wait_send()

    side = subs * K
    unit = jnp.where(
        lax.broadcasted_iota(jnp.int32, (side, side), 0)
        == lax.broadcasted_iota(jnp.int32, (side, side), 1),
        1.0,
        0.0,
    ).astype(BF16)

    def put(p):
        out_ref[:, p * K : (p + 1) * K] = dot_t(unit, gath[p])

    @pl.when(first)
    def _():
        layer_copy().wait_recv()
        theirs = jnp.concatenate([layer_x[h] for h in range(BND // LANES)], axis=1)
        for p in range(1, last):
            extra_take(p).wait_recv()
            extra_mix(p).wait_recv()
        for p in range(last):
            take, mixed = (take_x[p], mix_x[p]) if p else (take_s[last], mix_s[last])
            block = dot_t(picked(theirs, take), mixed)
            gath[last, :, p * K : (p + 1) * K] = block.astype(BF16)
        diag_copy().wait_recv()
        gath[last, :, last * K :] = diag_r[...]
        put(0)
        put(last)
        for p in range(1, last):
            row_copy(p, p).wait_recv()
            put(p)

    @pl.when(jnp.logical_not(first))
    def _():
        for p in range(subs):

            @pl.when(p != me)
            def _():
                row_copy(p, p).wait_recv()

        out_ref[...] = dot_t(unit, jnp.concatenate([gath[p] for p in range(subs)], axis=0))

    @pl.when(jnp.logical_and(lead, me == last))
    def _():
        layer_copy().wait_send()
        diag_copy().wait_send()

    @pl.when(jnp.logical_and(lead, jnp.logical_and(me > 0, me < last)))
    def _():
        extra_take(me).wait_send()
        extra_mix(me).wait_send()

    for p in range(subs):
        direct = p != me
        if p == 0:
            direct = jnp.logical_and(direct, jnp.logical_not(jnp.logical_and(lead, me == last)))

        @pl.when(direct)
        def _():
            row_copy(me, p).wait_send()


def emit(matrix, crossed, matrix_hbm, crossed_hbm, sem):
    copies = [
        pltpu.make_async_copy(matrix, matrix_hbm, sem.at[0]),
        pltpu.make_async_copy(crossed, crossed_hbm, sem.at[1]),
    ]
    for c in copies:
        c.start()
    for c in copies:
        c.wait()


def per_device(
    eigvecs,
    local_blocks,
    local_cols,
    margin_rows,
    margin_lens,
    peer_blocks,
    peer_rowblocks,
    cross_blocks,
    cross_rowblocks,
):
    subs = lax.axis_size("sub")
    grps = lax.axis_size("grp")
    z = eigvecs[0, 0]
    lb = jnp.transpose(local_blocks[0, 0], (1, 0, 2))
    cols = jnp.transpose(local_cols[0], (2, 0, 1))
    nblk = z.shape[0]
    nnz = lb.shape[0]
    pb = peer_blocks[0, 0]
    cb = cross_blocks[0, 0]
    vmem = pl.BlockSpec(memory_space=pltpu.VMEM)
    hbm = pl.BlockSpec(memory_space=pltpu.HBM)
    dma = pltpu.SemaphoreType.DMA
    group_matrix, crossed = pl.pallas_call(
        functools.partial(kernel, subs, grps),
        out_shape=(
            pltpu.VMEM((subs * K, subs * K), F32),
            pltpu.VMEM((2, K, K), F32),
        ),
        in_specs=[hbm] * 9,
        out_specs=(vmem, vmem),
        scratch_shapes=[
            pltpu.SMEM(cols.shape, jnp.int32),
            pltpu.VMEM(margin_rows.shape[2:], jnp.int32),
            pltpu.SMEM((1, subs), jnp.int32),
            pltpu.SMEM(peer_rowblocks.shape[2:], jnp.int32),
            pltpu.SMEM(cross_rowblocks.shape[2:], jnp.int32),
            pltpu.VMEM(z.shape, BF16),
            pltpu.VMEM(lb.shape, BF16),
            pltpu.VMEM(pb.shape, BF16),
            pltpu.VMEM(cb.shape, BF16),
            pltpu.VMEM((K // 2 * nblk, LANES), F32),
            pltpu.VMEM((nblk * K, LANES), F32),
            pltpu.VMEM((nnz * 32 * (nblk + 8), LANES), F32),
            pltpu.VMEM(((subs - 1) * 256, LANES), F32),
            pltpu.VMEM((512, LANES), F32),
            pltpu.VMEM((nblk, K, LANES), BF16),
            pltpu.VMEM((nblk // 2, K, LANES), BF16),
            pltpu.VMEM((subs, 1, CAP), jnp.int32),
            pltpu.VMEM((subs, 1, CAP), jnp.int32),
            pltpu.VMEM((subs, K, CAP), BF16),
            pltpu.VMEM((subs, K, CAP), BF16),
            pltpu.VMEM((2, K, LANES), BF16),
            pltpu.VMEM((K, nblk * HALF), BF16),
            pltpu.VMEM((K, nblk * HALF), BF16),
            pltpu.VMEM((subs, K, CAP), BF16),
            pltpu.VMEM((subs, K, subs * K), BF16),
            pltpu.VMEM((subs, 1, CAP), jnp.int32),
            pltpu.VMEM((subs, K, CAP), BF16),
            pltpu.VMEM((BND // LANES, K, LANES), BF16),
            pltpu.VMEM((K, K), BF16),
            pltpu.VMEM((K, K), BF16),
            dma((8,)),
            dma((nnz,)),
            dma((subs,)),
            dma((subs,)),
            dma((subs,)),
            dma((subs,)),
            dma((2,)),
            dma((2,)),
            dma((subs,)),
            dma((subs,)),
            dma((subs,)),
            dma((subs,)),
            dma((6,)),
            pltpu.SemaphoreType.REGULAR,
        ],
        compiler_params=pltpu.CompilerParams(
            collective_id=0, has_side_effects=True, vmem_limit_bytes=40 * 1024 * 1024
        ),
    )(
        *[
            pltpu.with_memory_space_constraint(x, pltpu.HBM)
            for x in (
                z,
                lb,
                pb,
                cb,
                cols,
                margin_rows[0, 0],
                margin_lens[0],
                peer_rowblocks[0, 0],
                cross_rowblocks[0, 0],
            )
        ]
    )
    group_matrix, crossed = pl.pallas_call(
        emit,
        out_shape=(
            jax.ShapeDtypeStruct(group_matrix.shape, F32),
            jax.ShapeDtypeStruct(crossed.shape, F32),
        ),
        in_specs=[vmem, vmem],
        out_specs=(hbm, hbm),
        scratch_shapes=[dma((2,))],
        compiler_params=pltpu.CompilerParams(vmem_limit_bytes=1024 * 1024),
    )(*[pltpu.with_memory_space_constraint(x, pltpu.VMEM) for x in (group_matrix, crossed)])
    return group_matrix[None], crossed[None, None]


def solution(mesh):
    return jax.shard_map(
        per_device,
        mesh=mesh,
        in_specs=(
            P("grp", "sub", None, None),
            P("grp", "sub", None, None, None),
            P("grp", "sub", None, None),
            P("grp", "sub", None, None),
            P("grp", "sub", None),
            P("grp", "sub", None, None, None),
            P("grp", "sub", None, None),
            P("grp", "sub", None, None, None),
            P("grp", "sub", None, None),
        ),
        out_specs=(P("grp", None, None), P("grp", "sub", None, None, None)),
        check_vma=False,
    )
```

```python
import functools

import jax
import jax.numpy as jnp
from jax import lax
from jax.experimental import pallas as pl
from jax.experimental.pallas import tpu as pltpu
from jax.sharding import PartitionSpec as P

K = 48
BND = 512
CAP = 256
FACE = 128
LANES = 128
HALF = 64
MESH = pl.DeviceIdType.MESH
F32 = jnp.float32
BF16 = jnp.bfloat16


def dot_t(a, b):
    return lax.dot_general(a, b, (((1,), (1,)), ((), ())), preferred_element_type=F32)


def dot(a, b):
    return lax.dot_general(a, b, (((1,), (0,)), ((), ())), preferred_element_type=F32)


def kernel(
    subs,
    grps,
    z_hbm,
    lb_hbm,
    pb_hbm,
    cb_hbm,
    cols_hbm,
    rows_hbm,
    lens_hbm,
    prow_hbm,
    crow_hbm,
    out_ref,
    cross_ref,
    cols,
    rows_ref,
    lens,
    prow,
    crow,
    z_v,
    lb_v,
    pb_v,
    cb_v,
    zf,
    zi,
    lf,
    pf,
    cf,
    zz,
    zpair,
    take_s,
    take_r,
    mix_s,
    mix_r,
    face,
    a_all,
    d_all,
    got,
    gath,
    take_x,
    mix_x,
    layer_x,
    diag_s,
    diag_r,
    in_sem,
    lb_sem,
    ts_sem,
    tr_sem,
    ls_sem,
    lr_sem,
    fs_sem,
    fr_sem,
    rs_sem,
    rr_sem,
    xt_sem,
    xm_sem,
    one_sem,
    ready,
):
    me = lax.axis_index("sub")
    g = lax.axis_index("grp")
    nblk = z_v.shape[0]
    nnz = lb_v.shape[0]
    pairs = nblk // 2
    step = nblk + 8
    ncb = CAP // 64
    nfb = FACE // 64
    last = subs - 1
    peers = [lax.rem(me + d, subs) for d in range(subs - 1, 0, -1)]
    sides = (g > 0).astype(jnp.int32) + (g < grps - 1).astype(jnp.int32)
    lead = g == 0
    first = jnp.logical_and(lead, me == 0)
    waits = last + sides - first.astype(jnp.int32)

    z_in = pltpu.make_async_copy(z_hbm, z_v, in_sem.at[0])
    z_in.start()
    barrier = pltpu.get_barrier_semaphore()
    below = g > 0
    above = g < grps - 1
    for p in range(subs):
        greet = p != me
        if p == 0:
            greet = jnp.logical_and(greet, jnp.logical_not(jnp.logical_and(lead, me == last)))

        @pl.when(greet)
        def _():
            pl.semaphore_signal(barrier, inc=1, device_id={"sub": p}, device_id_type=MESH)

    @pl.when(below)
    def _():
        pl.semaphore_signal(barrier, inc=1, device_id={"grp": g - 1}, device_id_type=MESH)

    @pl.when(above)
    def _():
        pl.semaphore_signal(barrier, inc=1, device_id={"grp": g + 1}, device_id_type=MESH)

    pb_in = pltpu.make_async_copy(pb_hbm, pb_v, in_sem.at[1])
    pb_in.start()
    cb_in = pltpu.make_async_copy(cb_hbm, cb_v, in_sem.at[2])
    cb_in.start()
    small_in = [
        pltpu.make_async_copy(a, b, in_sem.at[3 + i])
        for i, (a, b) in enumerate(
            [
                (prow_hbm, prow),
                (lens_hbm, lens),
                (rows_hbm, rows_ref),
                (cols_hbm, cols),
                (crow_hbm, crow),
            ]
        )
    ]
    for c in small_in:
        c.start()
    lb_in = [pltpu.make_async_copy(lb_hbm.at[t], lb_v.at[t], lb_sem.at[t]) for t in range(nnz)]
    for t in range(nnz):
        lb_in[t].start()

    lane = lax.broadcasted_iota(jnp.int32, (1, LANES), 1)
    lo = lane < HALF

    z_in.wait()
    for q in range(K // 2):
        zf[q * nblk : (q + 1) * nblk, :] = z_v[:, q * LANES : (q + 1) * LANES].astype(F32)

    def z_body(i, carry):
        for s in range(2):
            r = i * 2 + s
            v = zf[pl.ds(r, K // 2, stride=nblk), :]
            w = pltpu.roll(v, HALF, 1)
            zi[pl.ds(r * K, K // 2, stride=2), :] = jnp.where(lo, v, w)
            zi[pl.ds(r * K + 1, K // 2, stride=2), :] = jnp.where(lo, w, v)
        a = zi[pl.ds(i * 2 * K, K), :]
        b = zi[pl.ds(i * 2 * K + K, K), :]
        zz[i * 2] = a.astype(BF16)
        zz[i * 2 + 1] = b.astype(BF16)
        zpair[i] = jnp.where(lo, a, b).astype(BF16)
        return carry

    lax.fori_loop(0, pairs, z_body, 0, unroll=4)

    src = lax.broadcasted_iota(jnp.int32, (LANES, LANES), 0)
    dst = lax.broadcasted_iota(jnp.int32, (LANES, LANES), 1) % HALF
    want = jnp.where(dst < 32, dst * 2, (dst - 32) * 2 + 1)
    sel = jnp.where(src == want, 1.0, 0.0).astype(BF16)

    def take_copy(mine, theirs, peer):
        return pltpu.make_async_remote_copy(
            src_ref=take_s.at[mine],
            dst_ref=take_r.at[theirs],
            send_sem=ts_sem.at[mine],
            recv_sem=tr_sem.at[theirs],
            device_id={"sub": peer},
            device_id_type=MESH,
        )

    def mix_copy(mine, theirs, peer):
        return pltpu.make_async_remote_copy(
            src_ref=mix_s.at[mine],
            dst_ref=mix_r.at[theirs],
            send_sem=ls_sem.at[mine],
            recv_sem=lr_sem.at[theirs],
            device_id={"sub": peer},
            device_id_type=MESH,
        )

    def extra_take(slot):
        return pltpu.make_async_remote_copy(
            src_ref=take_s.at[last],
            dst_ref=take_x.at[slot],
            send_sem=one_sem.at[0],
            recv_sem=xt_sem.at[slot],
            device_id={"sub": 0},
            device_id_type=MESH,
        )

    def extra_mix(slot):
        return pltpu.make_async_remote_copy(
            src_ref=mix_s.at[last],
            dst_ref=mix_x.at[slot],
            send_sem=one_sem.at[1],
            recv_sem=xm_sem.at[slot],
            device_id={"sub": 0},
            device_id_type=MESH,
        )

    def layer_copy():
        return pltpu.make_async_remote_copy(
            src_ref=zpair.at[pl.ds(0, BND // LANES)],
            dst_ref=layer_x,
            send_sem=one_sem.at[2],
            recv_sem=one_sem.at[3],
            device_id={"sub": 0},
            device_id_type=MESH,
        )

    def diag_copy():
        return pltpu.make_async_remote_copy(
            src_ref=diag_s,
            dst_ref=diag_r,
            send_sem=one_sem.at[4],
            recv_sem=one_sem.at[5],
            device_id={"sub": 0},
            device_id_type=MESH,
        )

    for c in small_in:
        c.wait()
    slots = lax.broadcasted_iota(jnp.int32, (1, CAP), 1)
    for peer in peers:
        take_s[peer] = jnp.where(slots < lens[0, peer], rows_ref[pl.ds(peer, 1), :], -1)
    mix_r[me] = jnp.zeros((K, CAP), BF16)

    @pl.when(me == last)
    def _():
        pl.semaphore_wait(barrier, waits)

        @pl.when(lead)
        def _():
            pl.semaphore_signal(ready, inc=1, device_id={"sub": 0}, device_id_type=MESH)

        for p in range(last):
            take_copy(p, last, p).start()

    pb_in.wait()

    def unfold(x0, x1):
        x0, x1 = x0.astype(BF16), x1.astype(BF16)
        e = jnp.where(lo, x0, pltpu.roll(x1, HALF, 1))
        o = jnp.where(lo, pltpu.roll(x0, HALF, 1), x1)
        return jnp.concatenate([e, o], axis=0)

    def mix(x0, x1, r0, r1):
        both = dot(jnp.concatenate([zz[r0], zz[r1]], axis=0), sel).astype(BF16)[:, :HALF]
        m = dot(both, unfold(x0, x1))
        return jnp.where(lo, m[:K], m[K:]).astype(BF16)

    for n, peer in enumerate(peers):
        for m in range(32):
            pf[n * 256 + m * 8 : n * 256 + m * 8 + ncb, :] = pb_v[
                peer, :, m * LANES : (m + 1) * LANES
            ].astype(F32)
    for n, peer in enumerate(peers):
        for c in range(0, ncb, 2):
            x0 = pf[pl.ds(n * 256 + c, 32, stride=8), :]
            x1 = pf[pl.ds(n * 256 + c + 1, 32, stride=8), :]
            mix_s[peer, :, c * HALF : (c + 2) * HALF] = mix(
                x0, x1, prow[peer, c], prow[peer, c + 1]
            )

    @pl.when(me == last)
    def _():
        for p in [*range(1, last), 0]:
            mix_copy(p, last, p).start()

        @pl.when(lead)
        def _():
            layer_copy().start()

    @pl.when(me != last)
    def _():
        pl.semaphore_wait(barrier, waits)
        sends = [*range(1, last), last, 0]
        between = jnp.logical_and(lead, me > 0)

        @pl.when(between)
        def _():
            extra_take(me).start()

        for copy in (take_copy, mix_copy):
            for p in sends:

                now = p != me
                if p == last:
                    now = jnp.logical_and(now, jnp.logical_not(first))

                @pl.when(now)
                def _():
                    copy(p, me, p).start()

        @pl.when(between)
        def _():
            extra_mix(me).start()

    def face_copy(side, target):
        return pltpu.make_async_remote_copy(
            src_ref=zpair.at[BND // LANES + 1 - side],
            dst_ref=face.at[side],
            send_sem=fs_sem.at[side],
            recv_sem=fr_sem.at[side],
            device_id={"grp": target},
            device_id_type=MESH,
        )

    @pl.when(above)
    def _():
        face_copy(0, g + 1).start()

    @pl.when(below)
    def _():
        face_copy(1, g - 1).start()


    for t in range(nnz):
        lb_in[t].wait()

    def l_body(t, carry):
        for m in range(32):
            lf[pl.ds((t * 32 + m) * step, nblk), :] = lb_v[
                t, :, m * LANES : (m + 1) * LANES
            ].astype(F32)
        return carry

    lax.fori_loop(0, nnz, l_body, 0)

    zero = jnp.zeros((32, LANES), F32)

    def own_part(r):
        weights, moving = [], []
        for t in range(0, nnz, 2):
            x0 = lf[pl.ds(t * 32 * step + r, 32, stride=step), :]
            if t + 1 < nnz:
                x1 = lf[pl.ds((t + 1) * 32 * step + r, 32, stride=step), :]
                vec = jnp.where(lo, zz[cols[t, 0, r]], zz[cols[t + 1, 0, r]])
            else:
                x1 = zero
                vec = zz[cols[t, 0, r]]
            weights.append(unfold(x0, x1))
            moving.append(vec)
        return dot_t(jnp.concatenate(moving, axis=1), jnp.concatenate(weights, axis=1))

    def r_body(i, carry):
        at = pl.multiple_of(i * LANES, LANES)
        moved = dot(jnp.concatenate([zz[i * 2], zz[i * 2 + 1]], axis=0), sel)
        d_all[:, pl.ds(at, LANES)] = jnp.where(lo, moved[:K], moved[K:]).astype(BF16)
        a = own_part(i * 2)
        b = own_part(i * 2 + 1)
        a_all[:, pl.ds(at, LANES)] = jnp.concatenate(
            [a, b], axis=1
        ).astype(BF16)
        return carry

    lax.fori_loop(0, pairs, r_body, 0, unroll=16)
    own = dot_t(a_all[...], d_all[...])

    def picked(cells_of, take):
        cells = lax.broadcasted_iota(jnp.int32, (BND, CAP), 0)
        hot = jnp.where(cells == take, 1.0, 0.0).astype(BF16)
        return dot(cells_of, hot).astype(BF16)

    @pl.when(jnp.logical_and(lead, me == last))
    def _():
        diag_s[...] = own.astype(BF16)
        diag_copy().start()

    @pl.when(first)
    def _():
        pl.semaphore_wait(ready, 1)
        take_copy(last, 0, last).start()
        mix_copy(last, 0, last).start()

    layer = jnp.concatenate([zpair[h] for h in range(BND // LANES)], axis=1)
    got[me] = jnp.zeros((K, CAP), BF16)

    def row_copy(slot, peer):
        return pltpu.make_async_remote_copy(
            src_ref=gath.at[slot],
            dst_ref=gath.at[slot],
            send_sem=rs_sem.at[peer],
            recv_sem=rr_sem.at[slot],
            device_id={"sub": peer},
            device_id_type=MESH,
        )

    for p in [*range(1, last), 0, last]:
        @pl.when(p != me)
        def _():
            take_copy(p, p, p).wait_recv()
            got[p] = picked(layer, take_r[p])
            mix_copy(p, p, p).wait_recv()

        block = dot_t(got[p], mix_r[p]) + jnp.where(p == me, 1.0, 0.0) * own
        gath[me, :, p * K : (p + 1) * K] = block.astype(BF16)

    for p in range(subs):
        direct = p != me
        if p == 0:
            direct = jnp.logical_and(direct, jnp.logical_not(jnp.logical_and(lead, me == last)))

        @pl.when(direct)
        def _():
            row_copy(me, p).start()

    @pl.when(g > 0)
    def _():
        face_copy(0, g + 1).wait_recv()

    @pl.when(g == 0)
    def _():
        face[0] = jnp.zeros((K, LANES), BF16)

    @pl.when(g < grps - 1)
    def _():
        face_copy(1, g - 1).wait_recv()

    @pl.when(g == grps - 1)
    def _():
        face[1] = jnp.zeros((K, LANES), BF16)

    cb_in.wait()
    for q in range(2):
        for m in range(32):
            cf[q * 256 + m * 8 : q * 256 + m * 8 + nfb, :] = cb_v[
                q, :, m * LANES : (m + 1) * LANES
            ].astype(F32)
        x0 = cf[pl.ds(q * 256, 32, stride=8), :]
        x1 = cf[pl.ds(q * 256 + 1, 32, stride=8), :]
        mixed = mix(x0, x1, crow[q, 0], crow[q, 1])
        cross_ref[q] = dot_t(mixed, face[q])

    @pl.when(g < grps - 1)
    def _():
        face_copy(0, g + 1).wait_send()

    @pl.when(g > 0)
    def _():
        face_copy(1, g - 1).wait_send()

    for peer in peers:
        take_copy(peer, me, peer).wait_send()
        mix_copy(peer, me, peer).wait_send()

    side = subs * K
    unit = jnp.where(
        lax.broadcasted_iota(jnp.int32, (side, side), 0)
        == lax.broadcasted_iota(jnp.int32, (side, side), 1),
        1.0,
        0.0,
    ).astype(BF16)

    def put(p):
        out_ref[:, p * K : (p + 1) * K] = dot_t(unit, gath[p])

    @pl.when(first)
    def _():
        layer_copy().wait_recv()
        theirs = jnp.concatenate([layer_x[h] for h in range(BND // LANES)], axis=1)
        for p in range(1, last):
            extra_take(p).wait_recv()
            extra_mix(p).wait_recv()
        for p in range(last):
            take, mixed = (take_x[p], mix_x[p]) if p else (take_s[last], mix_s[last])
            block = dot_t(picked(theirs, take), mixed)
            gath[last, :, p * K : (p + 1) * K] = block.astype(BF16)
        diag_copy().wait_recv()
        gath[last, :, last * K :] = diag_r[...]
        put(0)
        put(last)
        for p in range(1, last):
            row_copy(p, p).wait_recv()
            put(p)

    @pl.when(jnp.logical_not(first))
    def _():
        for p in range(subs):

            @pl.when(p != me)
            def _():
                row_copy(p, p).wait_recv()

        out_ref[...] = dot_t(unit, jnp.concatenate([gath[p] for p in range(subs)], axis=0))

    @pl.when(jnp.logical_and(lead, me == last))
    def _():
        layer_copy().wait_send()
        diag_copy().wait_send()

    @pl.when(jnp.logical_and(lead, jnp.logical_and(me > 0, me < last)))
    def _():
        extra_take(me).wait_send()
        extra_mix(me).wait_send()

    for p in range(subs):
        direct = p != me
        if p == 0:
            direct = jnp.logical_and(direct, jnp.logical_not(jnp.logical_and(lead, me == last)))

        @pl.when(direct)
        def _():
            row_copy(me, p).wait_send()


def emit(matrix, crossed, matrix_hbm, crossed_hbm, sem):
    copies = [
        pltpu.make_async_copy(matrix, matrix_hbm, sem.at[0]),
        pltpu.make_async_copy(crossed, crossed_hbm, sem.at[1]),
    ]
    for c in copies:
        c.start()
    for c in copies:
        c.wait()


def per_device(
    eigvecs,
    local_blocks,
    local_cols,
    margin_rows,
    margin_lens,
    peer_blocks,
    peer_rowblocks,
    cross_blocks,
    cross_rowblocks,
):
    subs = lax.axis_size("sub")
    grps = lax.axis_size("grp")
    z = eigvecs[0, 0]
    lb = jnp.transpose(local_blocks[0, 0], (1, 0, 2))
    cols = jnp.transpose(local_cols[0], (2, 0, 1))
    nblk = z.shape[0]
    nnz = lb.shape[0]
    pb = peer_blocks[0, 0]
    cb = cross_blocks[0, 0]
    vmem = pl.BlockSpec(memory_space=pltpu.VMEM)
    hbm = pl.BlockSpec(memory_space=pltpu.HBM)
    dma = pltpu.SemaphoreType.DMA
    group_matrix, crossed = pl.pallas_call(
        functools.partial(kernel, subs, grps),
        out_shape=(
            pltpu.VMEM((subs * K, subs * K), F32),
            pltpu.VMEM((2, K, K), F32),
        ),
        in_specs=[hbm] * 9,
        out_specs=(vmem, vmem),
        scratch_shapes=[
            pltpu.SMEM(cols.shape, jnp.int32),
            pltpu.VMEM(margin_rows.shape[2:], jnp.int32),
            pltpu.SMEM((1, subs), jnp.int32),
            pltpu.SMEM(peer_rowblocks.shape[2:], jnp.int32),
            pltpu.SMEM(cross_rowblocks.shape[2:], jnp.int32),
            pltpu.VMEM(z.shape, BF16),
            pltpu.VMEM(lb.shape, BF16),
            pltpu.VMEM(pb.shape, BF16),
            pltpu.VMEM(cb.shape, BF16),
            pltpu.VMEM((K // 2 * nblk, LANES), F32),
            pltpu.VMEM((nblk * K, LANES), F32),
            pltpu.VMEM((nnz * 32 * (nblk + 8), LANES), F32),
            pltpu.VMEM(((subs - 1) * 256, LANES), F32),
            pltpu.VMEM((512, LANES), F32),
            pltpu.VMEM((nblk, K, LANES), BF16),
            pltpu.VMEM((nblk // 2, K, LANES), BF16),
            pltpu.VMEM((subs, 1, CAP), jnp.int32),
            pltpu.VMEM((subs, 1, CAP), jnp.int32),
            pltpu.VMEM((subs, K, CAP), BF16),
            pltpu.VMEM((subs, K, CAP), BF16),
            pltpu.VMEM((2, K, LANES), BF16),
            pltpu.VMEM((K, nblk * HALF), BF16),
            pltpu.VMEM((K, nblk * HALF), BF16),
            pltpu.VMEM((subs, K, CAP), BF16),
            pltpu.VMEM((subs, K, subs * K), BF16),
            pltpu.VMEM((subs, 1, CAP), jnp.int32),
            pltpu.VMEM((subs, K, CAP), BF16),
            pltpu.VMEM((BND // LANES, K, LANES), BF16),
            pltpu.VMEM((K, K), BF16),
            pltpu.VMEM((K, K), BF16),
            dma((8,)),
            dma((nnz,)),
            dma((subs,)),
            dma((subs,)),
            dma((subs,)),
            dma((subs,)),
            dma((2,)),
            dma((2,)),
            dma((subs,)),
            dma((subs,)),
            dma((subs,)),
            dma((subs,)),
            dma((6,)),
            pltpu.SemaphoreType.REGULAR,
        ],
        compiler_params=pltpu.CompilerParams(
            collective_id=0, has_side_effects=True, vmem_limit_bytes=40 * 1024 * 1024
        ),
    )(
        *[
            pltpu.with_memory_space_constraint(x, pltpu.HBM)
            for x in (
                z,
                lb,
                pb,
                cb,
                cols,
                margin_rows[0, 0],
                margin_lens[0],
                peer_rowblocks[0, 0],
                cross_rowblocks[0, 0],
            )
        ]
    )
    group_matrix, crossed = pl.pallas_call(
        emit,
        out_shape=(
            jax.ShapeDtypeStruct(group_matrix.shape, F32),
            jax.ShapeDtypeStruct(crossed.shape, F32),
        ),
        in_specs=[vmem, vmem],
        out_specs=(hbm, hbm),
        scratch_shapes=[dma((2,))],
        compiler_params=pltpu.CompilerParams(vmem_limit_bytes=1024 * 1024),
    )(*[pltpu.with_memory_space_constraint(x, pltpu.VMEM) for x in (group_matrix, crossed)])
    return group_matrix[None], crossed[None, None]


def solution(mesh):
    return jax.shard_map(
        per_device,
        mesh=mesh,
        in_specs=(
            P("grp", "sub", None, None),
            P("grp", "sub", None, None, None),
            P("grp", "sub", None, None),
            P("grp", "sub", None, None),
            P("grp", "sub", None),
            P("grp", "sub", None, None, None),
            P("grp", "sub", None, None),
            P("grp", "sub", None, None, None),
            P("grp", "sub", None, None),
        ),
        out_specs=(P("grp", None, None), P("grp", "sub", None, None, None)),
        check_vma=False,
    )
```

```python
import functools

import jax
import jax.numpy as jnp
from jax import lax
from jax.experimental import pallas as pl
from jax.experimental.pallas import tpu as pltpu
from jax.sharding import PartitionSpec as P

K = 48
BND = 512
CAP = 256
FACE = 128
LANES = 128
HALF = 64
MESH = pl.DeviceIdType.MESH
F32 = jnp.float32
BF16 = jnp.bfloat16


def dot_t(a, b):
    return lax.dot_general(a, b, (((1,), (1,)), ((), ())), preferred_element_type=F32)


def dot(a, b):
    return lax.dot_general(a, b, (((1,), (0,)), ((), ())), preferred_element_type=F32)


def kernel(
    subs,
    grps,
    z_hbm,
    lb_hbm,
    pb_hbm,
    cb_hbm,
    cols_hbm,
    rows_hbm,
    lens_hbm,
    prow_hbm,
    crow_hbm,
    out_ref,
    cross_ref,
    cols,
    rows_ref,
    lens,
    prow,
    crow,
    z_v,
    lb_v,
    pb_v,
    cb_v,
    zf,
    zi,
    lf,
    pf,
    cf,
    zz,
    zpair,
    take_s,
    take_r,
    mix_s,
    mix_r,
    face,
    a_all,
    d_all,
    got,
    gath,
    take_x,
    mix_x,
    layer_x,
    diag_s,
    diag_r,
    in_sem,
    lb_sem,
    ts_sem,
    tr_sem,
    ls_sem,
    lr_sem,
    fs_sem,
    fr_sem,
    rs_sem,
    rr_sem,
    xt_sem,
    xm_sem,
    one_sem,
    ready,
):
    me = lax.axis_index("sub")
    g = lax.axis_index("grp")
    nblk = z_v.shape[0]
    nnz = lb_v.shape[0]
    pairs = nblk // 2
    step = nblk + 8
    ncb = CAP // 64
    nfb = FACE // 64
    last = subs - 1
    peers = [lax.rem(me + d, subs) for d in range(subs - 1, 0, -1)]
    sides = (g > 0).astype(jnp.int32) + (g < grps - 1).astype(jnp.int32)
    lead = g == 0
    first = jnp.logical_and(lead, me == 0)
    ahead = jnp.logical_and(lead, me != last)
    waits = last + sides - ahead.astype(jnp.int32)

    z_in = pltpu.make_async_copy(z_hbm, z_v, in_sem.at[0])
    z_in.start()
    barrier = pltpu.get_barrier_semaphore()
    below = g > 0
    above = g < grps - 1
    for p in range(subs):
        greet = jnp.logical_not(jnp.logical_and(lead, me == last))

        @pl.when(jnp.logical_and(p != me, greet))
        def _():
            pl.semaphore_signal(barrier, inc=1, device_id={"sub": p}, device_id_type=MESH)

    @pl.when(below)
    def _():
        pl.semaphore_signal(barrier, inc=1, device_id={"grp": g - 1}, device_id_type=MESH)

    @pl.when(above)
    def _():
        pl.semaphore_signal(barrier, inc=1, device_id={"grp": g + 1}, device_id_type=MESH)

    pb_in = pltpu.make_async_copy(pb_hbm, pb_v, in_sem.at[1])
    pb_in.start()
    cb_in = pltpu.make_async_copy(cb_hbm, cb_v, in_sem.at[2])
    cb_in.start()
    small_in = [
        pltpu.make_async_copy(a, b, in_sem.at[3 + i])
        for i, (a, b) in enumerate(
            [
                (prow_hbm, prow),
                (lens_hbm, lens),
                (rows_hbm, rows_ref),
                (cols_hbm, cols),
                (crow_hbm, crow),
            ]
        )
    ]
    for c in small_in:
        c.start()
    lb_in = [pltpu.make_async_copy(lb_hbm.at[t], lb_v.at[t], lb_sem.at[t]) for t in range(nnz)]
    for t in range(nnz):
        lb_in[t].start()

    lane = lax.broadcasted_iota(jnp.int32, (1, LANES), 1)
    lo = lane < HALF

    z_in.wait()
    for q in range(K // 2):
        zf[q * nblk : (q + 1) * nblk, :] = z_v[:, q * LANES : (q + 1) * LANES].astype(F32)

    def z_body(i, carry):
        for s in range(2):
            r = i * 2 + s
            v = zf[pl.ds(r, K // 2, stride=nblk), :]
            w = pltpu.roll(v, HALF, 1)
            zi[pl.ds(r * K, K // 2, stride=2), :] = jnp.where(lo, v, w)
            zi[pl.ds(r * K + 1, K // 2, stride=2), :] = jnp.where(lo, w, v)
        a = zi[pl.ds(i * 2 * K, K), :]
        b = zi[pl.ds(i * 2 * K + K, K), :]
        zz[i * 2] = a.astype(BF16)
        zz[i * 2 + 1] = b.astype(BF16)
        zpair[i] = jnp.where(lo, a, b).astype(BF16)
        return carry

    lax.fori_loop(0, pairs, z_body, 0, unroll=4)

    src = lax.broadcasted_iota(jnp.int32, (LANES, LANES), 0)
    dst = lax.broadcasted_iota(jnp.int32, (LANES, LANES), 1) % HALF
    want = jnp.where(dst < 32, dst * 2, (dst - 32) * 2 + 1)
    sel = jnp.where(src == want, 1.0, 0.0).astype(BF16)

    def take_copy(mine, theirs, peer):
        return pltpu.make_async_remote_copy(
            src_ref=take_s.at[mine],
            dst_ref=take_r.at[theirs],
            send_sem=ts_sem.at[mine],
            recv_sem=tr_sem.at[theirs],
            device_id={"sub": peer},
            device_id_type=MESH,
        )

    def mix_copy(mine, theirs, peer):
        return pltpu.make_async_remote_copy(
            src_ref=mix_s.at[mine],
            dst_ref=mix_r.at[theirs],
            send_sem=ls_sem.at[mine],
            recv_sem=lr_sem.at[theirs],
            device_id={"sub": peer},
            device_id_type=MESH,
        )

    def extra_take(slot):
        return pltpu.make_async_remote_copy(
            src_ref=take_s.at[last],
            dst_ref=take_x.at[slot],
            send_sem=one_sem.at[0],
            recv_sem=xt_sem.at[slot],
            device_id={"sub": 0},
            device_id_type=MESH,
        )

    def extra_mix(slot):
        return pltpu.make_async_remote_copy(
            src_ref=mix_s.at[last],
            dst_ref=mix_x.at[slot],
            send_sem=one_sem.at[1],
            recv_sem=xm_sem.at[slot],
            device_id={"sub": 0},
            device_id_type=MESH,
        )

    def layer_copy():
        return pltpu.make_async_remote_copy(
            src_ref=zpair.at[pl.ds(0, BND // LANES)],
            dst_ref=layer_x,
            send_sem=one_sem.at[2],
            recv_sem=one_sem.at[3],
            device_id={"sub": 0},
            device_id_type=MESH,
        )

    def diag_copy():
        return pltpu.make_async_remote_copy(
            src_ref=diag_s,
            dst_ref=diag_r,
            send_sem=one_sem.at[4],
            recv_sem=one_sem.at[5],
            device_id={"sub": 0},
            device_id_type=MESH,
        )

    for c in small_in:
        c.wait()
    slots = lax.broadcasted_iota(jnp.int32, (1, CAP), 1)
    for peer in peers:
        take_s[peer] = jnp.where(slots < lens[0, peer], rows_ref[pl.ds(peer, 1), :], -1)
    mix_r[me] = jnp.zeros((K, CAP), BF16)

    @pl.when(me == last)
    def _():
        pl.semaphore_wait(barrier, waits)

        @pl.when(lead)
        def _():
            for p in range(last):
                pl.semaphore_signal(ready, inc=1, device_id={"sub": p}, device_id_type=MESH)

        for p in range(last):
            take_copy(p, last, p).start()

    pb_in.wait()

    def unfold(x0, x1):
        x0, x1 = x0.astype(BF16), x1.astype(BF16)
        e = jnp.where(lo, x0, pltpu.roll(x1, HALF, 1))
        o = jnp.where(lo, pltpu.roll(x0, HALF, 1), x1)
        return jnp.concatenate([e, o], axis=0)

    def mix(x0, x1, r0, r1):
        both = dot(jnp.concatenate([zz[r0], zz[r1]], axis=0), sel).astype(BF16)[:, :HALF]
        m = dot(both, unfold(x0, x1))
        return jnp.where(lo, m[:K], m[K:]).astype(BF16)

    for n, peer in enumerate(peers):
        for m in range(32):
            pf[n * 256 + m * 8 : n * 256 + m * 8 + ncb, :] = pb_v[
                peer, :, m * LANES : (m + 1) * LANES
            ].astype(F32)
    for n, peer in enumerate(peers):
        for c in range(0, ncb, 2):
            x0 = pf[pl.ds(n * 256 + c, 32, stride=8), :]
            x1 = pf[pl.ds(n * 256 + c + 1, 32, stride=8), :]
            mix_s[peer, :, c * HALF : (c + 2) * HALF] = mix(
                x0, x1, prow[peer, c], prow[peer, c + 1]
            )

    @pl.when(me == last)
    def _():
        for p in [*range(1, last), 0]:
            mix_copy(p, last, p).start()

        @pl.when(lead)
        def _():
            layer_copy().start()

    @pl.when(me != last)
    def _():
        pl.semaphore_wait(barrier, waits)
        sends = [last, *range(1, last), 0]
        between = jnp.logical_and(lead, me > 0)

        for copy in (take_copy, mix_copy):
            for p in sends:

                now = p != me
                if p == last:
                    now = jnp.logical_and(now, jnp.logical_not(lead))

                @pl.when(now)
                def _():
                    copy(p, me, p).start()

        @pl.when(between)
        def _():
            extra_take(me).start()
            extra_mix(me).start()

    def face_copy(side, target):
        return pltpu.make_async_remote_copy(
            src_ref=zpair.at[BND // LANES + 1 - side],
            dst_ref=face.at[side],
            send_sem=fs_sem.at[side],
            recv_sem=fr_sem.at[side],
            device_id={"grp": target},
            device_id_type=MESH,
        )

    @pl.when(above)
    def _():
        face_copy(0, g + 1).start()

    @pl.when(below)
    def _():
        face_copy(1, g - 1).start()


    for t in range(nnz):
        lb_in[t].wait()

    def l_body(t, carry):
        for m in range(32):
            lf[pl.ds((t * 32 + m) * step, nblk), :] = lb_v[
                t, :, m * LANES : (m + 1) * LANES
            ].astype(F32)
        return carry

    lax.fori_loop(0, nnz, l_body, 0)

    zero = jnp.zeros((32, LANES), F32)

    def own_part(r):
        weights, moving = [], []
        for t in range(0, nnz, 2):
            x0 = lf[pl.ds(t * 32 * step + r, 32, stride=step), :]
            if t + 1 < nnz:
                x1 = lf[pl.ds((t + 1) * 32 * step + r, 32, stride=step), :]
                vec = jnp.where(lo, zz[cols[t, 0, r]], zz[cols[t + 1, 0, r]])
            else:
                x1 = zero
                vec = zz[cols[t, 0, r]]
            weights.append(unfold(x0, x1))
            moving.append(vec)
        return dot_t(jnp.concatenate(moving, axis=1), jnp.concatenate(weights, axis=1))

    def r_body(i, carry):
        at = pl.multiple_of(i * LANES, LANES)
        moved = dot(jnp.concatenate([zz[i * 2], zz[i * 2 + 1]], axis=0), sel)
        d_all[:, pl.ds(at, LANES)] = jnp.where(lo, moved[:K], moved[K:]).astype(BF16)
        a = own_part(i * 2)
        b = own_part(i * 2 + 1)
        a_all[:, pl.ds(at, LANES)] = jnp.concatenate(
            [a, b], axis=1
        ).astype(BF16)
        return carry

    lax.fori_loop(0, pairs, r_body, 0, unroll=16)
    own = dot_t(a_all[...], d_all[...])

    def picked(cells_of, take):
        cells = lax.broadcasted_iota(jnp.int32, (BND, CAP), 0)
        hot = jnp.where(cells == take, 1.0, 0.0).astype(BF16)
        return dot(cells_of, hot).astype(BF16)

    @pl.when(jnp.logical_and(lead, me == last))
    def _():
        diag_s[...] = own.astype(BF16)
        diag_copy().start()

    @pl.when(ahead)
    def _():
        pl.semaphore_wait(ready, 1)
        take_copy(last, me, last).start()
        mix_copy(last, me, last).start()

    layer = jnp.concatenate([zpair[h] for h in range(BND // LANES)], axis=1)
    got[me] = jnp.zeros((K, CAP), BF16)

    def row_copy(slot, peer):
        return pltpu.make_async_remote_copy(
            src_ref=gath.at[slot],
            dst_ref=gath.at[slot],
            send_sem=rs_sem.at[peer],
            recv_sem=rr_sem.at[slot],
            device_id={"sub": peer},
            device_id_type=MESH,
        )

    for p in [*range(1, last), 0, last]:
        @pl.when(p != me)
        def _():
            take_copy(p, p, p).wait_recv()
            got[p] = picked(layer, take_r[p])
            mix_copy(p, p, p).wait_recv()

        block = dot_t(got[p], mix_r[p]) + jnp.where(p == me, 1.0, 0.0) * own
        gath[me, :, p * K : (p + 1) * K] = block.astype(BF16)

    for p in range(subs):
        direct = p != me
        if p == 0:
            direct = jnp.logical_and(direct, jnp.logical_not(jnp.logical_and(lead, me == last)))

        @pl.when(direct)
        def _():
            row_copy(me, p).start()

    @pl.when(g > 0)
    def _():
        face_copy(0, g + 1).wait_recv()

    @pl.when(g == 0)
    def _():
        face[0] = jnp.zeros((K, LANES), BF16)

    @pl.when(g < grps - 1)
    def _():
        face_copy(1, g - 1).wait_recv()

    @pl.when(g == grps - 1)
    def _():
        face[1] = jnp.zeros((K, LANES), BF16)

    cb_in.wait()
    for q in range(2):
        for m in range(32):
            cf[q * 256 + m * 8 : q * 256 + m * 8 + nfb, :] = cb_v[
                q, :, m * LANES : (m + 1) * LANES
            ].astype(F32)
        x0 = cf[pl.ds(q * 256, 32, stride=8), :]
        x1 = cf[pl.ds(q * 256 + 1, 32, stride=8), :]
        mixed = mix(x0, x1, crow[q, 0], crow[q, 1])
        cross_ref[q] = dot_t(mixed, face[q])

    @pl.when(g < grps - 1)
    def _():
        face_copy(0, g + 1).wait_send()

    @pl.when(g > 0)
    def _():
        face_copy(1, g - 1).wait_send()

    for peer in peers:
        take_copy(peer, me, peer).wait_send()
        mix_copy(peer, me, peer).wait_send()

    side = subs * K
    unit = jnp.where(
        lax.broadcasted_iota(jnp.int32, (side, side), 0)
        == lax.broadcasted_iota(jnp.int32, (side, side), 1),
        1.0,
        0.0,
    ).astype(BF16)

    def put(p):
        out_ref[:, p * K : (p + 1) * K] = dot_t(unit, gath[p])

    @pl.when(first)
    def _():
        layer_copy().wait_recv()
        theirs = jnp.concatenate([layer_x[h] for h in range(BND // LANES)], axis=1)
        for p in range(1, last):
            extra_take(p).wait_recv()
            extra_mix(p).wait_recv()
        for p in range(last):
            take, mixed = (take_x[p], mix_x[p]) if p else (take_s[last], mix_s[last])
            block = dot_t(picked(theirs, take), mixed)
            gath[last, :, p * K : (p + 1) * K] = block.astype(BF16)
        diag_copy().wait_recv()
        gath[last, :, last * K :] = diag_r[...]
        put(0)
        put(last)
        for p in range(1, last):
            row_copy(p, p).wait_recv()
            put(p)

    @pl.when(jnp.logical_not(first))
    def _():
        for p in range(subs):

            @pl.when(p != me)
            def _():
                row_copy(p, p).wait_recv()

        out_ref[...] = dot_t(unit, jnp.concatenate([gath[p] for p in range(subs)], axis=0))

    @pl.when(jnp.logical_and(lead, me == last))
    def _():
        layer_copy().wait_send()
        diag_copy().wait_send()

    @pl.when(jnp.logical_and(lead, jnp.logical_and(me > 0, me < last)))
    def _():
        extra_take(me).wait_send()
        extra_mix(me).wait_send()

    for p in range(subs):
        direct = p != me
        if p == 0:
            direct = jnp.logical_and(direct, jnp.logical_not(jnp.logical_and(lead, me == last)))

        @pl.when(direct)
        def _():
            row_copy(me, p).wait_send()


def emit(matrix, crossed, matrix_hbm, crossed_hbm, sem):
    copies = [
        pltpu.make_async_copy(matrix, matrix_hbm, sem.at[0]),
        pltpu.make_async_copy(crossed, crossed_hbm, sem.at[1]),
    ]
    for c in copies:
        c.start()
    for c in copies:
        c.wait()


def per_device(
    eigvecs,
    local_blocks,
    local_cols,
    margin_rows,
    margin_lens,
    peer_blocks,
    peer_rowblocks,
    cross_blocks,
    cross_rowblocks,
):
    subs = lax.axis_size("sub")
    grps = lax.axis_size("grp")
    z = eigvecs[0, 0]
    lb = jnp.transpose(local_blocks[0, 0], (1, 0, 2))
    cols = jnp.transpose(local_cols[0], (2, 0, 1))
    nblk = z.shape[0]
    nnz = lb.shape[0]
    pb = peer_blocks[0, 0]
    cb = cross_blocks[0, 0]
    vmem = pl.BlockSpec(memory_space=pltpu.VMEM)
    hbm = pl.BlockSpec(memory_space=pltpu.HBM)
    dma = pltpu.SemaphoreType.DMA
    group_matrix, crossed = pl.pallas_call(
        functools.partial(kernel, subs, grps),
        out_shape=(
            pltpu.VMEM((subs * K, subs * K), F32),
            pltpu.VMEM((2, K, K), F32),
        ),
        in_specs=[hbm] * 9,
        out_specs=(vmem, vmem),
        scratch_shapes=[
            pltpu.SMEM(cols.shape, jnp.int32),
            pltpu.VMEM(margin_rows.shape[2:], jnp.int32),
            pltpu.SMEM((1, subs), jnp.int32),
            pltpu.SMEM(peer_rowblocks.shape[2:], jnp.int32),
            pltpu.SMEM(cross_rowblocks.shape[2:], jnp.int32),
            pltpu.VMEM(z.shape, BF16),
            pltpu.VMEM(lb.shape, BF16),
            pltpu.VMEM(pb.shape, BF16),
            pltpu.VMEM(cb.shape, BF16),
            pltpu.VMEM((K // 2 * nblk, LANES), F32),
            pltpu.VMEM((nblk * K, LANES), F32),
            pltpu.VMEM((nnz * 32 * (nblk + 8), LANES), F32),
            pltpu.VMEM(((subs - 1) * 256, LANES), F32),
            pltpu.VMEM((512, LANES), F32),
            pltpu.VMEM((nblk, K, LANES), BF16),
            pltpu.VMEM((nblk // 2, K, LANES), BF16),
            pltpu.VMEM((subs, 1, CAP), jnp.int32),
            pltpu.VMEM((subs, 1, CAP), jnp.int32),
            pltpu.VMEM((subs, K, CAP), BF16),
            pltpu.VMEM((subs, K, CAP), BF16),
            pltpu.VMEM((2, K, LANES), BF16),
            pltpu.VMEM((K, nblk * HALF), BF16),
            pltpu.VMEM((K, nblk * HALF), BF16),
            pltpu.VMEM((subs, K, CAP), BF16),
            pltpu.VMEM((subs, K, subs * K), BF16),
            pltpu.VMEM((subs, 1, CAP), jnp.int32),
            pltpu.VMEM((subs, K, CAP), BF16),
            pltpu.VMEM((BND // LANES, K, LANES), BF16),
            pltpu.VMEM((K, K), BF16),
            pltpu.VMEM((K, K), BF16),
            dma((8,)),
            dma((nnz,)),
            dma((subs,)),
            dma((subs,)),
            dma((subs,)),
            dma((subs,)),
            dma((2,)),
            dma((2,)),
            dma((subs,)),
            dma((subs,)),
            dma((subs,)),
            dma((subs,)),
            dma((6,)),
            pltpu.SemaphoreType.REGULAR,
        ],
        compiler_params=pltpu.CompilerParams(
            collective_id=0, has_side_effects=True, vmem_limit_bytes=40 * 1024 * 1024
        ),
    )(
        *[
            pltpu.with_memory_space_constraint(x, pltpu.HBM)
            for x in (
                z,
                lb,
                pb,
                cb,
                cols,
                margin_rows[0, 0],
                margin_lens[0],
                peer_rowblocks[0, 0],
                cross_rowblocks[0, 0],
            )
        ]
    )
    group_matrix, crossed = pl.pallas_call(
        emit,
        out_shape=(
            jax.ShapeDtypeStruct(group_matrix.shape, F32),
            jax.ShapeDtypeStruct(crossed.shape, F32),
        ),
        in_specs=[vmem, vmem],
        out_specs=(hbm, hbm),
        scratch_shapes=[dma((2,))],
        compiler_params=pltpu.CompilerParams(vmem_limit_bytes=1024 * 1024),
    )(*[pltpu.with_memory_space_constraint(x, pltpu.VMEM) for x in (group_matrix, crossed)])
    return group_matrix[None], crossed[None, None]


def solution(mesh):
    return jax.shard_map(
        per_device,
        mesh=mesh,
        in_specs=(
            P("grp", "sub", None, None),
            P("grp", "sub", None, None, None),
            P("grp", "sub", None, None),
            P("grp", "sub", None, None),
            P("grp", "sub", None),
            P("grp", "sub", None, None, None),
            P("grp", "sub", None, None),
            P("grp", "sub", None, None, None),
            P("grp", "sub", None, None),
        ),
        out_specs=(P("grp", None, None), P("grp", "sub", None, None, None)),
        check_vma=False,
    )
```
